32 devices in a mesh: row: 4 (over y, core), col: 8 (over z, x).
Axes of the slice: x: 2, y: 2, z: 4, core: 2. Of those that a mesh axis runs over, the one named last changes fastest.
Arguments:
- tokens: bfloat16 [1024, 4096], P('row', 'col'), may hold values from -6 to 6
- gate_weight: bfloat16 [4096, 16384], P('row', 'col'), may hold values from -0.1875 to 0.1875
- up_weight: bfloat16 [4096, 16384], P('row', 'col'), may hold values from -0.1875 to 0.1875
- gate_mask: int32 [32, 128], P('row', 'col'), may hold values from 0 to 1, as said below
- up_mask: int32 [32, 128], P('row', 'col'), may hold values from 0 to 1, as said below
- cotangent: bfloat16 [1024, 16384], P('row', 'col'), may hold values from -6 to 6
Outputs:
- hidden: bfloat16 [1024, 16384], P('row', 'col')
- grad_tokens: bfloat16 [1024, 4096], P('row', 'col')
- grad_gate: bfloat16 [4096, 16384], P('row', 'col')
- grad_up: bfloat16 [4096, 16384], P('row', 'col')
The draws below stay inside these ranges and needn't reach their ends.
Inputs may be any that keep to these rules, and one draw needn't show every extreme that they name: `gate_mask`: blocks are aligned 128 x 128 squares; each device's tile of 8 x 16 blocks keeps between 16 and 32 of them, and some tile keeps exactly 32. `up_mask`: as for gate_mask, drawn independently.
All inputs are finite; a program needn't handle non-finite values.
Results may differ from the reference program's by a relative error of at most 0.022.
Values may be sent and summed in bfloat16 or wider, within the bound.
A program may use at most 128 MiB of HBM per device.

```python
import jax
import jax.numpy as jnp
from jax import lax

D = 4096
FF = 16384
BLK = 128
TOK_ROW = 256
TOKENS = 1024
N_ROW = 4
N_COL = 8


def block_pattern(key):
    row_blocks = D // (N_ROW * BLK)
    col_blocks = FF // (N_COL * BLK)
    per_tile = row_blocks * col_blocks
    tile_count = N_ROW * N_COL
    key_order, key_score = jax.random.split(key)
    order = jax.random.permutation(key_order, tile_count)
    counts = per_tile // 8 + order % (per_tile // 8 + 1)
    scores = jax.random.randint(key_score, (tile_count, per_tile), 0, 1 << 20) * per_tile
    scores = scores + jnp.arange(per_tile, dtype=jnp.int32)[None, :]
    order_rank = jnp.argsort(jnp.argsort(scores, axis=1), axis=1)
    keep = (order_rank < counts[:, None]).astype(jnp.int32)
    keep = keep.reshape(N_ROW, N_COL, row_blocks, col_blocks).transpose(0, 2, 1, 3)
    return keep.reshape(N_ROW * row_blocks, N_COL * col_blocks)


def draw_gate_mask(key, part):
    key = jax.random.fold_in(key, 11)
    return block_pattern(key)


def draw_up_mask(key, part):
    key = jax.random.fold_in(key, 23)
    return block_pattern(key)


def steps_of(own_key, shape, pieces, least, high):
    factor_of, own = 1.0, jax.random.fold_in(own_key, 6)
    for position, blocks in pieces:
        draws = jnp.exp(jax.random.uniform(jax.random.fold_in(own, position), (blocks,), jnp.float32, least / len(pieces), high / len(pieces)))
        factor_of = factor_of * jnp.repeat(draws, shape[position] // blocks).reshape([-1 if axis == position else 1 for axis in range(len(shape))])
    return factor_of


def gaussian(rng, extent, deviation, reach, cuts=(), held_as=jnp.bfloat16):
    result = jax.random.normal(rng, extent, jnp.float32) * deviation
    if len(cuts) > 0:
        result = steps_of(rng, extent, cuts, -0.22, 0.18) * result
    return jnp.clip(result, min=-reach, max=reach).astype(held_as)


def setup_inputs(seed: int = 0) -> dict:
    key_list = jax.random.split(jax.random.key(seed), 7)
    return {
        "tokens": gaussian(key_list[0], (TOKENS, D), 1.0, 6.0, ((0, 4), (1, 8))),
        "gate_weight": gaussian(key_list[1], (D, FF), (D // 4) ** -0.5, 0.1875, ((0, 4), (1, 8))),
        "up_weight": gaussian(key_list[2], (D, FF), (D // 4) ** -0.5, 0.1875, ((0, 4), (1, 8))),
        "gate_mask": draw_gate_mask(jax.random.fold_in(key_list[6], 71), 0),
        "up_mask": draw_up_mask(jax.random.fold_in(key_list[6], 71), 0),
        "cotangent": gaussian(key_list[5], (TOKENS, FF), 1.0, 6.0, ((0, 4), (1, 8))),
    }


def expand_mask(block_mask):
    return jnp.repeat(jnp.repeat(block_mask, BLK, axis=0), BLK, axis=1)


def reference(tokens, gate_weight, up_weight, gate_mask, up_mask, cotangent):
    gate_full = expand_mask(gate_mask)
    up_full = expand_mask(up_mask)
    gate_eff = gate_weight * gate_full.astype(jnp.bfloat16)
    up_eff = up_weight * up_full.astype(jnp.bfloat16)
    gate_value = jnp.dot(tokens, gate_eff, preferred_element_type=jnp.float32)
    up_value = jnp.dot(tokens, up_eff, preferred_element_type=jnp.float32)
    sigma = jax.nn.sigmoid(gate_value)
    hidden = (gate_value * sigma * up_value).astype(jnp.bfloat16)
    cot = cotangent.astype(jnp.float32)
    grad_gval = (cot * up_value * sigma * (1.0 + gate_value * (1.0 - sigma))).astype(jnp.bfloat16)
    grad_uval = (cot * gate_value * sigma).astype(jnp.bfloat16)

    width = FF // N_COL

    def col_step(total, index):
        offset = (index * width).astype(jnp.int32)
        part_g = lax.dynamic_slice_in_dim(grad_gval, offset, width, 1)
        part_u = lax.dynamic_slice_in_dim(grad_uval, offset, width, 1)
        weight_g = lax.dynamic_slice_in_dim(gate_eff, offset, width, 1)
        weight_u = lax.dynamic_slice_in_dim(up_eff, offset, width, 1)
        term = jnp.dot(part_g, weight_g.T, preferred_element_type=jnp.float32)
        term = term + jnp.dot(part_u, weight_u.T, preferred_element_type=jnp.float32)
        rounded = lax.optimization_barrier(term.astype(jnp.bfloat16))
        return total + rounded.astype(jnp.float32), None

    start_tokens = jnp.zeros((TOKENS, D), jnp.float32)
    total_tokens, _ = lax.scan(col_step, start_tokens, jnp.arange(N_COL, dtype=jnp.int32))
    grad_tokens = total_tokens.astype(jnp.bfloat16)

    def row_step(totals, index):
        offset = (index * TOK_ROW).astype(jnp.int32)
        rows_x = lax.dynamic_slice_in_dim(tokens, offset, TOK_ROW, 0)
        rows_g = lax.dynamic_slice_in_dim(grad_gval, offset, TOK_ROW, 0)
        rows_u = lax.dynamic_slice_in_dim(grad_uval, offset, TOK_ROW, 0)
        term_g = lax.optimization_barrier(jnp.dot(rows_x.T, rows_g, preferred_element_type=jnp.float32).astype(jnp.bfloat16))
        term_u = lax.optimization_barrier(jnp.dot(rows_x.T, rows_u, preferred_element_type=jnp.float32).astype(jnp.bfloat16))
        return (totals[0] + term_g.astype(jnp.float32), totals[1] + term_u.astype(jnp.float32)), None

    start_weights = (jnp.zeros((D, FF), jnp.float32), jnp.zeros((D, FF), jnp.float32))
    sums, _ = lax.scan(row_step, start_weights, jnp.arange(N_ROW, dtype=jnp.int32))
    grad_gate = (sums[0] * gate_full.astype(jnp.float32)).astype(jnp.bfloat16)
    grad_up = (sums[1] * up_full.astype(jnp.float32)).astype(jnp.bfloat16)
    return hidden, grad_tokens, grad_gate, grad_up
```

```python
import functools

import jax
import jax.numpy as jnp
from jax import lax
from jax.experimental import pallas as pl
from jax.experimental.pallas import tpu as pltpu
from jax.sharding import PartitionSpec as P

BLK = 128
MESH = pl.DeviceIdType.MESH
BF = jnp.bfloat16
F32 = jnp.float32


def tables(mask, capacity):
    flat = mask.reshape(-1)
    count = flat.shape[0]
    ids = jnp.arange(count, dtype=jnp.int32)
    before = jnp.sum(jnp.where(ids[None, :] < ids[:, None], flat[None, :], 0), axis=1)
    pos = jnp.where(flat == 1, before, capacity)
    slot = jnp.arange(BLK, dtype=jnp.int32)
    place = jnp.sum(jnp.where(pos[None, :] == slot[:, None], ids[None, :], 0), axis=1)
    place = jnp.where(slot < capacity, place, 0)
    cols = mask.shape[1]
    pos = jnp.pad(pos, (0, BLK - count), constant_values=capacity)
    return pos, place // cols, place % cols


def fused(
    dims, tok, gw, uw, tab, tab_s, cot, hid, gt, pg, pu,
    wt_g, wt_u, own_g, own_u, par_g, par_u, yg, yu, fg, fu, tabs_v, tabs,
    xb, xt, gv, uv, wch, wrow, gb_g, gb_u, gtr_g, gtr_u,
    sp, rp, sy, ry, sq, rq, ow, sx, rx, sz, rz,
    ldsem, lsem, tab_ss, tab_rs, xz_s, xz_r, xp_s, xp_r, wy_s, wy_r, wp_s, wp_r, wf_s, wf_r,
    dp_s, dp_r, dy_s, dy_r, dq_s, dq_r, tx_s, tx_r, tz_s, tz_r,
):
    n_row, n_col, rb, cb, cap, nkb, toks = dims
    n_y, n_a = n_row // 2, n_col // 2
    row, col = lax.axis_index("row"), lax.axis_index("col")
    y, core = row // 2, lax.rem(row, 2)
    a, b = col // 2, lax.rem(col, 2)
    mate = y * 2 + 1 - core
    side = a * 2 + 1 - b
    pairs = cb // 2

    def y_peer(k):
        return lax.rem(y + k, n_y) * 2 + core

    def z_peer(k):
        return lax.rem(a + k, n_a) * 2 + b

    def push(src, dst, ssem, rsem, r, c):
        return pltpu.make_async_remote_copy(
            src_ref=src, dst_ref=dst, send_sem=ssem, recv_sem=rsem,
            device_id=(r, c), device_id_type=MESH,
        )

    loads = [
        [
            pltpu.make_async_copy(src.at[:, :, pl.ds(nb * BLK, BLK)], wt.at[nb], ldsem.at[m, nb])
            for nb in range(cb)
        ]
        for m, (src, wt) in enumerate(((gw, wt_g), (uw, wt_u)))
    ]
    for c in loads[0] + loads[1]:
        c.start()

    barrier = pltpu.get_barrier_semaphore()
    for k in range(1, n_row):
        pl.semaphore_signal(barrier, inc=1, device_id=(lax.rem(row + k, n_row), col), device_id_type=MESH)
    for k in range(1, n_a):
        pl.semaphore_signal(barrier, inc=1, device_id=(row, z_peer(k)), device_id_type=MESH)
    pl.semaphore_signal(barrier, inc=1, device_id=(row, side), device_id_type=MESH)
    for i in range(nkb):
        xb[col * nkb + i] = tok[:, i * BLK:(i + 1) * BLK]
    tabs_v[row] = tab[...]
    pl.semaphore_wait(barrier, n_row - 1 + n_a)

    started = []

    tab_copies = []
    for k in range(1, n_row):
        c = push(tabs_v.at[row], tabs_v.at[row], tab_ss.at[k], tab_rs.at[k], lax.rem(row + k, n_row), col)
        c.start()
        tab_copies.append(c)
    started += tab_copies

    def shard(which):
        return xb.at[pl.ds(which * nkb, nkb)]

    xz = []
    for k in range(1, n_a):
        c = push(shard(col), shard(col), xz_s.at[k], xz_r.at[k], row, z_peer(k))
        c.start()
        xz.append(c)
    xp = [push(shard(col), shard(col), xp_s.at[0], xp_r.at[0], row, side)]
    xp[0].start()

    zero = jnp.zeros((BLK, BLK), BF)
    own, par, ys, fs_ = (own_g, own_u), (par_g, par_u), (yg, yu), (fg, fu)
    for m in range(2):
        own[m][0, cap] = zero
        par[m][0, cap] = zero
        for k in range(n_y - 1):
            ys[m][k, cap] = zero
            fs_[m][k, cap] = zero

    wy = [[], []]
    wp = []
    unroll = min(8, cap)
    for m, wt in enumerate((wt_g, wt_u)):
        for c in loads[m]:
            c.wait()

        def pack(i, _, m=m, wt=wt):
            for j in range(unroll):
                s = i * unroll + j
                own[m][0, s] = wt[tab_s[3 + 2 * m, s], tab_s[2 + 2 * m, s]]
            return 0

        lax.fori_loop(0, cap // unroll, pack, 0)
        mine = own[m].at[0, pl.ds(0, cap)]
        for k in range(1, n_y):
            c = push(mine, ys[m].at[k - 1, pl.ds(0, cap)], wy_s.at[m, k], wy_r.at[m, k], y_peer(k), col)
            c.start()
            wy[m].append(c)
        c = push(mine, par[m].at[0, pl.ds(0, cap)], wp_s.at[m], wp_r.at[m], mate, col)
        c.start()
        wp.append(c)

    for c in tab_copies:
        c.wait_recv()
    to_smem = pltpu.make_async_copy(tabs_v, tabs, lsem.at[0])
    to_smem.start()
    to_smem.wait()

    for k in range(1, n_a):
        xz[k - 1].wait_recv()
        source = lax.rem(a - k + n_a, n_a) * 2 + b
        c = push(shard(source), shard(source), xp_s.at[k], xp_r.at[k], row, side)
        c.start()
        xp.append(c)
    for c in xp:
        c.wait_recv()

    def forward(ref, lead, r, m, acc, first):
        def step(i, _):
            x = jnp.concatenate([xb[r * rb + kb] for kb in range(rb)], axis=1)
            for half in range(2):
                p = i * 2 + half
                for kb in range(rb):
                    for q in range(2):
                        slot = tabs[r, m, kb * cb + p * 2 + q]
                        wch[half, kb * BLK:(kb + 1) * BLK, q * BLK:(q + 1) * BLK] = ref[lead, slot]
                d = jnp.dot(x, wch[half], preferred_element_type=F32)
                if first:
                    acc[p] = d
                else:
                    acc[p] += d
            return 0

        lax.fori_loop(0, pairs // 2, step, 0)

    accs = (gv, uv)
    for m in range(2):
        forward(own[m], 0, row, m, accs[m], True)
    for m in range(2):
        wp[m].wait_recv()
        forward(par[m], 0, mate, m, accs[m], False)

    def transpose_x(i, _):
        xt[i] = xb[i].astype(F32).T.astype(BF)
        return 0

    lax.fori_loop(0, n_row * rb, transpose_x, 0)

    wf = [[], []]
    for m in range(2):
        for k in range(1, n_y):
            wy[m][k - 1].wait_recv()
            c = push(
                ys[m].at[k - 1, pl.ds(0, cap)], fs_[m].at[k - 1, pl.ds(0, cap)],
                wf_s.at[m, k], wf_r.at[m, k], mate, col,
            )
            c.start()
            wf[m].append(c)
        for k in range(1, n_y):
            source = lax.rem(y - k + n_y, n_y) * 2
            forward(ys[m], k - 1, source + core, m, accs[m], False)
        for c in wf[m]:
            c.wait_recv()
        for k in range(1, n_y):
            source = lax.rem(y - k + n_y, n_y) * 2
            forward(fs_[m], k - 1, source + 1 - core, m, accs[m], False)

    gbs, gtrs = (gb_g, gb_u), (gtr_g, gtr_u)

    def gates(p, _):
        g, u = gv[p], uv[p]
        at = pl.ds(pl.multiple_of(p * 2 * BLK, 2 * BLK), 2 * BLK)
        c = cot[:, at].astype(F32)
        s = jax.nn.sigmoid(g)
        gs = g * s
        hid[:, at] = (gs * u).astype(BF)
        dg = (c * u * s * (1.0 + g * (1.0 - s))).astype(BF)
        du = (c * gs).astype(BF)
        for grad, blocks, turned in ((dg, gb_g, gtr_g), (du, gb_u, gtr_u)):
            blocks[p * 2] = grad[:, :BLK]
            blocks[p * 2 + 1] = grad[:, BLK:]
            turned[at, :] = grad.astype(F32).T.astype(BF)
        return 0

    lax.fori_loop(0, pairs, gates, 0)

    def weight_grad(r, m, write):
        def step(i, _):
            for j in range(unroll):
                s = i * unroll + j
                kb, nb = tabs[r, 2 + 2 * m, s], tabs[r, 3 + 2 * m, s]
                write(s, jnp.dot(xt[r * rb + kb], gbs[m][nb], preferred_element_type=F32))
            return 0

        lax.fori_loop(0, cap // unroll, step, 0)

    dp = [[], []]
    for m in range(2):
        for k in range(1, n_y):
            def write(s, v, m=m, k=k):
                sp[m, k - 1, s] = v.astype(BF)

            weight_grad(lax.rem(y + k, n_y) * 2 + 1 - core, m, write)
            c = push(sp.at[m, k - 1], rp.at[m, k - 1], dp_s.at[m, k], dp_r.at[m, k], mate, col)
            c.start()
            dp[m].append(c)
    dy = [[], []]
    for m in range(2):
        for k in range(1, n_y):
            dp[m][k - 1].wait_recv()

            def write(s, v, m=m, k=k):
                sy[m, k - 1, s] = (v + rp[m, k - 1, s].astype(F32)).astype(BF)

            weight_grad(y_peer(k), m, write)
            c = push(sy.at[m, k - 1], ry.at[m, k - 1], dy_s.at[m, k], dy_r.at[m, k], y_peer(k), col)
            c.start()
            dy[m].append(c)

    tiles = [(own, 0, row), (par, 0, mate)]
    for k in range(1, n_y):
        source = lax.rem(y - k + n_y, n_y) * 2
        tiles.append((ys, k - 1, source + core))
        tiles.append((fs_, k - 1, source + 1 - core))
    span = min(2, nkb)

    def token_grad(refs, lead, r, half, write):
        def step(i, _):
            total = None
            for m in range(2):
                for q in range(span):
                    for nb in range(cb):
                        kb = half * nkb + i * span + q
                        slot = tabs[r, m, kb * cb + nb]
                        wrow[m, q * BLK:(q + 1) * BLK, nb * BLK:(nb + 1) * BLK] = refs[m][lead, slot]
                d = jnp.dot(wrow[m], gtrs[m][...], preferred_element_type=F32)
                total = d if total is None else total + d
            write(pl.ds(pl.multiple_of(i * span * BLK, span * BLK), span * BLK), total.T)
            return 0

        lax.fori_loop(0, nkb // span, step, 0)

    tx = []
    for refs, lead, r in tiles:
        def write(at, v, r=r):
            sx[r, :, at] = v.astype(BF)

        token_grad(refs, lead, r, 1 - b, write)
    for k in range(n_a):
        at = lax.rem(a + k, n_a)
        c = push(sx.at[at], rx.at[at], tx_s.at[k], tx_r.at[k], row, side)
        c.start()
        tx.append(c)

    dq = []
    for m in range(2):
        def write(s, v, m=m):
            sq[m, s] = v.astype(BF)

        weight_grad(mate, m, write)
        c = push(sq.at[m], rq.at[m], dq_s.at[m], dq_r.at[m], mate, col)
        c.start()
        dq.append(c)

    for c in tx:
        c.wait_recv()
    for refs, lead, r in tiles:
        def write(at, v, r=r):
            sz[r, :, at] = (v + rx[r, :, at].astype(F32)).astype(BF)

        token_grad(refs, lead, r, b, write)
    tz = []
    for k in range(1, n_a):
        c = push(sz.at[lax.rem(a + k, n_a)], rz.at[k - 1], tz_s.at[k], tz_r.at[k], row, z_peer(k))
        c.start()
        tz.append(c)

    for m in range(2):
        dq[m].wait_recv()

        def write(s, v, m=m):
            ow[m, s] = (v + rq[m, s].astype(F32)).astype(BF)

        weight_grad(row, m, write)

    for c in tz:
        c.wait_recv()
    total = sz[a].astype(F32)
    for k in range(n_a - 1):
        total = total + rz[k].astype(F32)
    gt[...] = total.astype(BF)

    for m, out in enumerate((pg, pu)):
        for c in dy[m]:
            c.wait_recv()

        def finish(s, _, m=m, out=out):
            v = ow[m, s].astype(F32)
            for k in range(n_y - 1):
                v = v + ry[m, k, s].astype(F32)
            out[s] = v.astype(BF)
            return 0

        lax.fori_loop(0, cap, finish, 0)

    for group in ([*tab_copies], xz, xp, wy[0], wy[1], wp, wf[0], wf[1], dp[0], dp[1], dy[0], dy[1], dq, tx, tz):
        for c in group:
            c.wait_send()


def expand(cb, tab_s, pg, pu, grad_g, grad_u):
    i = pl.program_id(0)
    for m, (packed, out) in enumerate(((pg, grad_g), (pu, grad_u))):
        cap = packed.shape[0]
        for nb in range(cb):
            slot = tab_s[m, i * cb + nb]
            block = packed[jnp.minimum(slot, cap - 1)]
            out[:, nb * BLK:(nb + 1) * BLK] = jnp.where(slot < cap, block, jnp.zeros_like(block))


def body(n_row, n_col, tokens, gate_weight, up_weight, gate_mask, up_mask, cotangent):
    rb, cb = gate_mask.shape
    cap = rb * cb // 4
    toks, feats = tokens.shape
    nkb = feats // BLK
    units = cb * BLK
    n_y, n_a = n_row // 2, n_col // 2
    assert n_col * nkb == n_row * rb and n_a == n_row and cb % 4 == 0
    pos_g, kb_g, nb_g = tables(gate_mask, cap)
    pos_u, kb_u, nb_u = tables(up_mask, cap)
    tab = jnp.stack([pos_g, pos_u, kb_g, nb_g, kb_u, nb_u, pos_g, pos_u])

    vm = pl.BlockSpec(memory_space=pltpu.VMEM)
    anyw = pl.BlockSpec(memory_space=pl.ANY)
    sm = pl.BlockSpec(memory_space=pltpu.SMEM)
    V, D = pltpu.VMEM, pltpu.SemaphoreType.DMA
    blocks = lambda *lead: V((*lead, BLK, BLK), BF)
    scratch = [
        blocks(cb, rb), blocks(cb, rb),
        blocks(1, cap + 1), blocks(1, cap + 1), blocks(1, cap + 1), blocks(1, cap + 1),
        blocks(n_y - 1, cap + 1), blocks(n_y - 1, cap + 1),
        blocks(n_y - 1, cap + 1), blocks(n_y - 1, cap + 1),
        V((n_row, 8, BLK), jnp.int32), pltpu.SMEM((n_row, 8, BLK), jnp.int32),
        V((n_row * rb, toks, BLK), BF), V((n_row * rb, BLK, toks), BF),
        V((cb // 2, toks, 2 * BLK), F32), V((cb // 2, toks, 2 * BLK), F32),
        V((2, rb * BLK, 2 * BLK), BF), V((2, min(2, nkb) * BLK, units), BF),
        V((cb, toks, BLK), BF), V((cb, toks, BLK), BF),
        V((units, toks), BF), V((units, toks), BF),
        blocks(2, n_y - 1, cap), blocks(2, n_y - 1, cap),
        blocks(2, n_y - 1, cap), blocks(2, n_y - 1, cap),
        blocks(2, cap), blocks(2, cap), blocks(2, cap),
        V((n_a, toks, feats), BF), V((n_a, toks, feats), BF),
        V((n_a, toks, feats), BF), V((n_a - 1, toks, feats), BF),
        D((2, cb)), D((1,)), D((n_row,)), D((n_row,)), D((n_a,)), D((n_a,)), D((n_a,)), D((n_a,)),
        D((2, n_y)), D((2, n_y)), D((2,)), D((2,)), D((2, n_y)), D((2, n_y)),
        D((2, n_y)), D((2, n_y)), D((2, n_y)), D((2, n_y)), D((2,)), D((2,)),
        D((n_a,)), D((n_a,)), D((n_a,)), D((n_a,)),
    ]
    dims = (n_row, n_col, rb, cb, cap, nkb, toks)
    hidden, grad_tokens, packed_g, packed_u = pl.pallas_call(
        functools.partial(fused, dims),
        out_shape=(
            jax.ShapeDtypeStruct((toks, units), BF),
            jax.ShapeDtypeStruct((toks, feats), BF),
            jax.ShapeDtypeStruct((cap, BLK, BLK), BF),
            jax.ShapeDtypeStruct((cap, BLK, BLK), BF),
        ),
        in_specs=[vm, anyw, anyw, vm, sm, vm],
        out_specs=(vm, vm, vm, vm),
        scratch_shapes=scratch,
        compiler_params=pltpu.CompilerParams(
            collective_id=0, has_side_effects=True, vmem_limit_bytes=62 * 1024 * 1024
        ),
        name="fused_layer",
    )(
        tokens, gate_weight.reshape(rb, BLK, units), up_weight.reshape(rb, BLK, units),
        tab, tab, cotangent,
    )

    whole = lambda i: (0, 0, 0)
    grad_gate, grad_up = pl.pallas_call(
        functools.partial(expand, cb),
        grid=(rb,),
        in_specs=[
            sm,
            pl.BlockSpec((cap, BLK, BLK), whole),
            pl.BlockSpec((cap, BLK, BLK), whole),
        ],
        out_specs=(
            pl.BlockSpec((BLK, units), lambda i: (i, 0)),
            pl.BlockSpec((BLK, units), lambda i: (i, 0)),
        ),
        out_shape=(
            jax.ShapeDtypeStruct((rb * BLK, units), BF),
            jax.ShapeDtypeStruct((rb * BLK, units), BF),
        ),
        name="expand_grads",
    )(tab, packed_g, packed_u)
    return hidden, grad_tokens, grad_gate, grad_up


def solution(mesh):
    spec = P("row", "col")
    return jax.shard_map(
        functools.partial(body, mesh.shape["row"], mesh.shape["col"]),
        mesh=mesh,
        in_specs=(spec,) * 6,
        out_specs=(spec,) * 4,
        check_vma=False,
    )
```

```python
import functools

import jax
import jax.numpy as jnp
from jax import lax
from jax.experimental import pallas as pl
from jax.experimental.pallas import tpu as pltpu
from jax.sharding import PartitionSpec as P

BLK = 128
MESH = pl.DeviceIdType.MESH
BF = jnp.bfloat16
F32 = jnp.float32


def write_table(mask_ref, table, row, m, rows, cap):
    rb, cb = mask_ref.shape
    mask = mask_ref[...]
    lane = lax.broadcasted_iota(jnp.int32, (rb, BLK), 1)
    sub = lax.broadcasted_iota(jnp.int32, (rb, BLK), 0)
    sub1 = lax.broadcasted_iota(jnp.int32, (rb, 1), 0)
    cols = [mask[:, nb:nb + 1] for nb in range(cb)]
    run = jnp.zeros((rb, 1), jnp.int32)
    before = []
    for c in cols:
        before.append(run)
        run = run + c
    offset = jnp.zeros((rb, 1), jnp.int32)
    for j in range(rb):
        offset = offset + jnp.where(sub1 > j, run[j:j + 1, :], 0)
    pos = jnp.full((rb, BLK), cap, jnp.int32)
    at_kb = jnp.zeros((rb, BLK), jnp.int32)
    at_nb = jnp.zeros((rb, BLK), jnp.int32)
    for nb, c in enumerate(cols):
        slot = jnp.where(c == 1, offset + before[nb], cap)
        pos = jnp.where(lane == nb, slot, pos)
        here = (lane == slot) & (lane < cap)
        at_kb = at_kb + jnp.where(here, sub, 0)
        at_nb = at_nb + jnp.where(here, nb, 0)
    table[row, m * rows:m * rows + rb, :] = pos
    base = 2 * rows + 2 * m
    table[row, base:base + 1, :] = jnp.sum(at_kb, axis=0, keepdims=True)
    table[row, base + 1:base + 2, :] = jnp.sum(at_nb, axis=0, keepdims=True)


def fused(
    dims, tok, gw, uw, gm, um, cot, hid, gt, pg, pu, tab_out,
    wt_g, wt_u, own_g, own_u, par_g, par_u, yg, yu, fg, fu, tabs_v, tab_s, tabs,
    xb, xt, gv, uv, wch, wrow, gb_g, gb_u, gtr_g, gtr_u,
    sp, rp, sy, ry, sq, rq, ow, sx, rx, sz, rz,
    ldsem, lsem, tab_ss, tab_rs, xz_s, xz_r, xp_s, xp_r, wy_s, wy_r, wp_s, wp_r, wf_s, wf_r,
    dp_s, dp_r, dy_s, dy_r, dq_s, dq_r, tx_s, tx_r, tz_s, tz_r,
):
    n_row, n_col, rb, cb, cap, nkb, toks = dims
    n_y, n_a = n_row // 2, n_col // 2
    rows = max(8, rb)
    row, col = lax.axis_index("row"), lax.axis_index("col")
    y, core = row // 2, lax.rem(row, 2)
    a, b = col // 2, lax.rem(col, 2)
    mate = y * 2 + 1 - core
    side = a * 2 + 1 - b
    pairs = cb // 2

    def y_peer(k):
        return lax.rem(y + k, n_y) * 2 + core

    def z_peer(k):
        return lax.rem(a + k, n_a) * 2 + b

    def push(src, dst, ssem, rsem, r, c):
        return pltpu.make_async_remote_copy(
            src_ref=src, dst_ref=dst, send_sem=ssem, recv_sem=rsem,
            device_id=(r, c), device_id_type=MESH,
        )

    loads = [
        [
            pltpu.make_async_copy(src.at[:, :, pl.ds(nb * BLK, BLK)], wt.at[nb], ldsem.at[m, nb])
            for nb in range(cb)
        ]
        for m, (src, wt) in enumerate(((gw, wt_g), (uw, wt_u)))
    ]
    for c in loads[0] + loads[1]:
        c.start()

    barrier = pltpu.get_barrier_semaphore()
    for k in range(1, n_row):
        pl.semaphore_signal(barrier, inc=1, device_id=(lax.rem(row + k, n_row), col), device_id_type=MESH)
    for k in range(1, n_a):
        pl.semaphore_signal(barrier, inc=1, device_id=(row, z_peer(k)), device_id_type=MESH)
    pl.semaphore_signal(barrier, inc=1, device_id=(row, side), device_id_type=MESH)
    for i in range(nkb):
        xb[col * nkb + i] = tok[:, i * BLK:(i + 1) * BLK]
    write_table(gm, tabs_v, row, 0, rows, cap)
    write_table(um, tabs_v, row, 1, rows, cap)
    own_tab = pltpu.make_async_copy(tabs_v.at[row], tab_s, lsem.at[1])
    own_tab.start()
    tab_out[...] = tabs_v[row]
    pl.semaphore_wait(barrier, n_row - 1 + n_a)

    tab_copies = []
    for k in range(1, n_row):
        c = push(tabs_v.at[row], tabs_v.at[row], tab_ss.at[k], tab_rs.at[k], lax.rem(row + k, n_row), col)
        c.start()
        tab_copies.append(c)

    def shard(which):
        return xb.at[pl.ds(which * nkb, nkb)]

    xz = []
    for k in range(1, n_a):
        c = push(shard(col), shard(col), xz_s.at[k], xz_r.at[k], row, z_peer(k))
        c.start()
        xz.append(c)
    xp = [push(shard(col), shard(col), xp_s.at[0], xp_r.at[0], row, side)]
    xp[0].start()

    zero = jnp.zeros((BLK, BLK), BF)
    own, par, ys, fs_ = (own_g, own_u), (par_g, par_u), (yg, yu), (fg, fu)
    for m in range(2):
        own[m][0, cap] = zero
        par[m][0, cap] = zero
        for k in range(n_y - 1):
            ys[m][k, cap] = zero
            fs_[m][k, cap] = zero

    own_tab.wait()
    wy = [[], []]
    wp = []
    unroll = min(8, cap)
    for m, wt in enumerate((wt_g, wt_u)):
        for c in loads[m]:
            c.wait()

        def pack(i, _, m=m, wt=wt):
            for j in range(unroll):
                s = i * unroll + j
                own[m][0, s] = wt[tab_s[2 * rows + 2 * m + 1, s], tab_s[2 * rows + 2 * m, s]]
            return 0

        lax.fori_loop(0, cap // unroll, pack, 0)
        mine = own[m].at[0, pl.ds(0, cap)]
        for k in range(1, n_y):
            c = push(mine, ys[m].at[k - 1, pl.ds(0, cap)], wy_s.at[m, k], wy_r.at[m, k], y_peer(k), col)
            wy[m].append(c)
            if m == 0:
                c.start()
        c = push(mine, par[m].at[0, pl.ds(0, cap)], wp_s.at[m], wp_r.at[m], mate, col)
        c.start()
        wp.append(c)

    for c in tab_copies:
        c.wait_recv()
    to_smem = pltpu.make_async_copy(tabs_v, tabs, lsem.at[0])
    to_smem.start()
    to_smem.wait()

    for k in range(1, n_a):
        xz[k - 1].wait_recv()
        source = lax.rem(a - k + n_a, n_a) * 2 + b
        c = push(shard(source), shard(source), xp_s.at[k], xp_r.at[k], row, side)
        c.start()
        xp.append(c)
    for c in wy[0]:
        c.wait_send()
    for c in wy[1]:
        c.start()
    for c in xp:
        c.wait_recv()

    def forward(ref, lead, r, m, acc, first):
        def step(i, _):
            x = jnp.concatenate([xb[r * rb + kb] for kb in range(rb)], axis=1)
            for half in range(2):
                p = i * 2 + half
                for kb in range(rb):
                    for q in range(2):
                        slot = tabs[r, m * rows + kb, p * 2 + q]
                        wch[half, kb * BLK:(kb + 1) * BLK, q * BLK:(q + 1) * BLK] = ref[lead, slot]
                d = jnp.dot(x, wch[half], preferred_element_type=F32)
                if first:
                    acc[p] = d
                else:
                    acc[p] += d
            return 0

        lax.fori_loop(0, pairs // 2, step, 0)

    accs = (gv, uv)
    gbs, gtrs = (gb_g, gb_u), (gtr_g, gtr_u)

    def transpose_x(i, _):
        xt[i] = xb[i].astype(F32).T.astype(BF)
        return 0

    def near(m):
        forward(own[m], 0, row, m, accs[m], True)
        wp[m].wait_recv()
        forward(par[m], 0, mate, m, accs[m], False)

    wf = [[], []]

    def far(m):
        for k in range(1, n_y):
            wy[m][k - 1].wait_recv()
            c = push(
                ys[m].at[k - 1, pl.ds(0, cap)], fs_[m].at[k - 1, pl.ds(0, cap)],
                wf_s.at[m, k], wf_r.at[m, k], mate, col,
            )
            c.start()
            wf[m].append(c)
        for k in range(1, n_y):
            source = lax.rem(y - k + n_y, n_y) * 2
            forward(ys[m], k - 1, source + core, m, accs[m], False)
        for c in wf[m]:
            c.wait_recv()
        for k in range(1, n_y):
            source = lax.rem(y - k + n_y, n_y) * 2
            forward(fs_[m], k - 1, source + 1 - core, m, accs[m], False)

    def units(p):
        return pl.ds(pl.multiple_of(p * 2 * BLK, 2 * BLK), 2 * BLK)

    def keep(grad, p, m):
        grad = grad.astype(BF)
        gbs[m][p * 2] = grad[:, :BLK]
        gbs[m][p * 2 + 1] = grad[:, BLK:]
        gtrs[m][units(p), :] = grad.astype(F32).T.astype(BF)

    def gates_up(p, _):
        g = gv[p]
        keep(cot[:, units(p)].astype(F32) * g * jax.nn.sigmoid(g), p, 1)
        return 0

    def gates_gate(p, _):
        g, u = gv[p], uv[p]
        s = jax.nn.sigmoid(g)
        hid[:, units(p)] = (g * s * u).astype(BF)
        keep(cot[:, units(p)].astype(F32) * u * s * (1.0 + g * (1.0 - s)), p, 0)
        return 0

    def weight_grad(r, m, write):
        def step(i, _):
            for j in range(unroll):
                s = i * unroll + j
                kb, nb = tabs[r, 2 * rows + 2 * m, s], tabs[r, 2 * rows + 2 * m + 1, s]
                write(s, jnp.dot(xt[r * rb + kb], gbs[m][nb], preferred_element_type=F32))
            return 0

        lax.fori_loop(0, cap // unroll, step, 0)

    dp, dy = [[], []], [[], []]

    def far_grad_mate(m):
        for k in range(1, n_y):
            def write(s, v):
                sp[m, k - 1, s] = v.astype(BF)

            weight_grad(lax.rem(y + k, n_y) * 2 + 1 - core, m, write)
            c = push(sp.at[m, k - 1], rp.at[m, k - 1], dp_s.at[m, k], dp_r.at[m, k], mate, col)
            c.start()
            dp[m].append(c)

    def far_grad(m):
        for k in range(1, n_y):
            dp[m][k - 1].wait_recv()

            def write(s, v):
                sy[m, k - 1, s] = (v + rp[m, k - 1, s].astype(F32)).astype(BF)

            weight_grad(y_peer(k), m, write)
            c = push(sy.at[m, k - 1], ry.at[m, k - 1], dy_s.at[m, k], dy_r.at[m, k], y_peer(k), col)
            dy[m].append(c)

    near(0)
    lax.fori_loop(0, n_row * rb, transpose_x, 0)
    far(0)
    lax.fori_loop(0, pairs, gates_up, 0)
    far_grad_mate(1)
    near(1)
    far_grad(1)
    for c in wy[1]:
        c.wait_send()
    for c in dy[1]:
        c.start()
    far(1)
    lax.fori_loop(0, pairs, gates_gate, 0)
    far_grad_mate(0)

    tiles = [(own, 0, row), (par, 0, mate)]
    for k in range(1, n_y):
        source = lax.rem(y - k + n_y, n_y) * 2
        tiles.append((ys, k - 1, source + core))
        tiles.append((fs_, k - 1, source + 1 - core))
    span = min(2, nkb)

    def token_grad(refs, lead, r, half, write):
        def step(i, _):
            total = None
            for m in range(2):
                for q in range(span):
                    for nb in range(cb):
                        kb = half * nkb + i * span + q
                        slot = tabs[r, m * rows + kb, nb]
                        wrow[m, q * BLK:(q + 1) * BLK, nb * BLK:(nb + 1) * BLK] = refs[m][lead, slot]
                d = jnp.dot(wrow[m], gtrs[m][...], preferred_element_type=F32)
                total = d if total is None else total + d
            write(pl.ds(pl.multiple_of(i * span * BLK, span * BLK), span * BLK), total.T)
            return 0

        lax.fori_loop(0, nkb // span, step, 0)

    tx = []
    for i, (refs, lead, r) in enumerate(tiles):
        def write(at, v, r=r):
            sx[r, :, at] = v.astype(BF)

        token_grad(refs, lead, r, 1 - b, write)
        c = push(sx.at[r], rx.at[r], tx_s.at[i], tx_r.at[i], row, side)
        c.start()
        tx.append(c)

    far_grad(0)
    for c in dy[0]:
        c.start()

    for i, (refs, lead, r) in enumerate(tiles):
        tx[i].wait_recv()

        def write(at, v, r=r):
            sz[r, :, at] = (v + rx[r, :, at].astype(F32)).astype(BF)

        token_grad(refs, lead, r, b, write)

        @pl.when(r != a)
        def _():
            k = lax.rem(r - a + n_a, n_a)
            push(sz.at[r], rz.at[k], tz_s.at[k], tz_r.at[k], lax.axis_index("row"), r * 2 + b).start()

    dq = []
    for m in (1, 0):
        def write(s, v):
            sq[m, s] = v.astype(BF)

        weight_grad(mate, m, write)
        c = push(sq.at[m], rq.at[m], dq_s.at[m], dq_r.at[m], mate, col)
        c.start()
        dq.append(c)
    for m, c in zip((1, 0), dq):
        c.wait_recv()

        def write(s, v):
            ow[m, s] = (v + rq[m, s].astype(F32)).astype(BF)

        weight_grad(row, m, write)

    def finish(m, out):
        out[cap] = zero
        for c in dy[m]:
            c.wait_recv()

        def step(s, _):
            v = ow[m, s].astype(F32)
            for k in range(n_y - 1):
                v = v + ry[m, k, s].astype(F32)
            out[s] = v.astype(BF)
            return 0

        lax.fori_loop(0, cap, step, 0)

    finish(1, pu)
    tz = [push(sz.at[z], rz.at[k], tz_s.at[k], tz_r.at[k], row, z * 2 + b)
          for k in range(1, n_a) for z in (lax.rem(a + k, n_a),)]
    total = sz[a].astype(F32)
    for k in range(1, n_a):
        tz[k - 1].wait_recv()
        total = total + rz[k].astype(F32)
    gt[...] = total.astype(BF)
    finish(0, pg)

    for group in (tab_copies, xz, xp, wp, wf[0], wf[1], dp[0], dp[1], dy[0], dy[1], dq, tx, tz):
        for c in group:
            c.wait_send()


def expand(cb, rows, tab_s, pg, pu, hid, gt, grad_g, grad_u, hid_out, gt_out, sem):
    i = pl.program_id(0)
    copies = [
        pltpu.make_async_copy(hid, hid_out, sem.at[0]),
        pltpu.make_async_copy(gt, gt_out, sem.at[1]),
    ]

    @pl.when(i == 0)
    def _():
        for c in copies:
            c.start()

    for m, (packed, out) in enumerate(((pg, grad_g), (pu, grad_u))):
        for nb in range(cb):
            out[:, nb * BLK:(nb + 1) * BLK] = packed[tab_s[m * rows + i, nb]]

    @pl.when(i == pl.num_programs(0) - 1)
    def _():
        for c in copies:
            c.wait()


def body(n_row, n_col, tokens, gate_weight, up_weight, gate_mask, up_mask, cotangent):
    rb, cb = gate_mask.shape
    cap = rb * cb // 4
    toks, feats = tokens.shape
    nkb = feats // BLK
    units = cb * BLK
    rows = max(8, rb)
    n_y, n_a = n_row // 2, n_col // 2
    assert n_col * nkb == n_row * rb and n_a == n_row and cb % 4 == 0

    vm = pl.BlockSpec(memory_space=pltpu.VMEM)
    anyw = pl.BlockSpec(memory_space=pl.ANY)
    sm = pl.BlockSpec(memory_space=pltpu.SMEM)
    V, D = pltpu.VMEM, pltpu.SemaphoreType.DMA
    blocks = lambda *lead: V((*lead, BLK, BLK), BF)
    scratch = [
        blocks(cb, rb), blocks(cb, rb),
        blocks(1, cap + 1), blocks(1, cap + 1), blocks(1, cap + 1), blocks(1, cap + 1),
        blocks(n_y - 1, cap + 1), blocks(n_y - 1, cap + 1),
        blocks(n_y - 1, cap + 1), blocks(n_y - 1, cap + 1),
        V((n_row, 2 * rows + 8, BLK), jnp.int32),
        pltpu.SMEM((2 * rows + 8, BLK), jnp.int32), pltpu.SMEM((n_row, 2 * rows + 8, BLK), jnp.int32),
        V((n_row * rb, toks, BLK), BF), V((n_row * rb, BLK, toks), BF),
        V((cb // 2, toks, 2 * BLK), F32), V((cb // 2, toks, 2 * BLK), F32),
        V((2, rb * BLK, 2 * BLK), BF), V((2, min(2, nkb) * BLK, units), BF),
        V((cb, toks, BLK), BF), V((cb, toks, BLK), BF),
        V((units, toks), BF), V((units, toks), BF),
        blocks(2, n_y - 1, cap), blocks(2, n_y - 1, cap),
        blocks(2, n_y - 1, cap), blocks(2, n_y - 1, cap),
        blocks(2, cap), blocks(2, cap), blocks(2, cap),
        V((n_a, toks, feats), BF), V((n_a, toks, feats), BF),
        V((n_a, toks, feats), BF), V((n_a, toks, feats), BF),
        D((2, cb)), D((2,)), D((n_row,)), D((n_row,)), D((n_a,)), D((n_a,)), D((n_a,)), D((n_a,)),
        D((2, n_y)), D((2, n_y)), D((2,)), D((2,)), D((2, n_y)), D((2, n_y)),
        D((2, n_y)), D((2, n_y)), D((2, n_y)), D((2, n_y)), D((2,)), D((2,)),
        D((n_a,)), D((n_a,)), D((n_a,)), D((n_a,)),
    ]
    dims = (n_row, n_col, rb, cb, cap, nkb, toks)
    packed = jax.ShapeDtypeStruct((cap + 1, BLK, BLK), BF)
    hidden_type = jax.ShapeDtypeStruct((toks, units), BF)
    tokens_type = jax.ShapeDtypeStruct((toks, feats), BF)
    weight_type = jax.ShapeDtypeStruct((rb * BLK, units), BF)
    hidden, grad_tokens, packed_g, packed_u, tab = pl.pallas_call(
        functools.partial(fused, dims),
        out_shape=(
            hidden_type, tokens_type, packed, packed,
            jax.ShapeDtypeStruct((2 * rows + 8, BLK), jnp.int32),
        ),
        in_specs=[vm, anyw, anyw, vm, vm, vm],
        out_specs=(vm, vm, vm, vm, vm),
        scratch_shapes=scratch,
        compiler_params=pltpu.CompilerParams(
            collective_id=0, has_side_effects=True, vmem_limit_bytes=62 * 1024 * 1024
        ),
        name="fused_layer",
    )(
        tokens, gate_weight.reshape(rb, BLK, units), up_weight.reshape(rb, BLK, units),
        gate_mask, up_mask, cotangent,
    )

    whole = pl.BlockSpec((cap + 1, BLK, BLK), lambda i: (0, 0, 0))
    strip = pl.BlockSpec((BLK, units), lambda i: (i, 0))
    grad_gate, grad_up, hidden, grad_tokens = pl.pallas_call(
        functools.partial(expand, cb, rows),
        grid=(rb,),
        in_specs=[sm, whole, whole, anyw, anyw],
        out_specs=(strip, strip, anyw, anyw),
        out_shape=(weight_type, weight_type, hidden_type, tokens_type),
        scratch_shapes=[D((2,))],
        name="expand_grads",
    )(tab, packed_g, packed_u, hidden, grad_tokens)
    return hidden, grad_tokens, grad_gate, grad_up


def solution(mesh):
    spec = P("row", "col")
    return jax.shard_map(
        functools.partial(body, mesh.shape["row"], mesh.shape["col"]),
        mesh=mesh,
        in_specs=(spec,) * 6,
        out_specs=(spec,) * 4,
        check_vma=False,
    )
```

```python
import functools

import jax
import jax.numpy as jnp
from jax import lax
from jax.experimental import pallas as pl
from jax.experimental.pallas import tpu as pltpu
from jax.sharding import PartitionSpec as P

BLK = 128
MESH = pl.DeviceIdType.MESH
BF = jnp.bfloat16
F32 = jnp.float32


def write_table(mask_ref, table, row, m, rows, cap):
    rb, cb = mask_ref.shape
    mask = mask_ref[...]
    lane = lax.broadcasted_iota(jnp.int32, (rb, BLK), 1)
    sub = lax.broadcasted_iota(jnp.int32, (rb, BLK), 0)
    sub1 = lax.broadcasted_iota(jnp.int32, (rb, 1), 0)
    cols = [mask[:, nb:nb + 1] for nb in range(cb)]
    run = jnp.zeros((rb, 1), jnp.int32)
    before = []
    for c in cols:
        before.append(run)
        run = run + c
    offset = jnp.zeros((rb, 1), jnp.int32)
    for j in range(rb):
        offset = offset + jnp.where(sub1 > j, run[j:j + 1, :], 0)
    pos = jnp.full((rb, BLK), cap, jnp.int32)
    at_kb = jnp.zeros((rb, BLK), jnp.int32)
    at_nb = jnp.zeros((rb, BLK), jnp.int32)
    for nb, c in enumerate(cols):
        slot = jnp.where(c == 1, offset + before[nb], cap)
        pos = jnp.where(lane == nb, slot, pos)
        here = (lane == slot) & (lane < cap)
        at_kb = at_kb + jnp.where(here, sub, 0)
        at_nb = at_nb + jnp.where(here, nb, 0)
    table[row, m * rows:m * rows + rb, :] = pos
    base = 2 * rows + 2 * m
    table[row, base:base + 1, :] = jnp.sum(at_kb, axis=0, keepdims=True)
    table[row, base + 1:base + 2, :] = jnp.sum(at_nb, axis=0, keepdims=True)


def fused(
    dims, tok, gw, uw, gm, um, cot_in, hid_out, gt, pg_out, pu_out, tab_out,
    wt_g, wt_u, own_g, own_u, par_g, par_u, yg, yu, fg, fu, tabs_v, tab_s, tabs,
    xb, xt, gv, uv, wch, wrow, gb_g, gb_u, gtr_g, gtr_u,
    cot, hid, pg, pu, sp, rp, sy, ry, sq, rq, ow, sx, rx, sz, rz,
    ldsem, lsem, tab_ss, tab_rs, xz_s, xz_r, xp_s, xp_r, wy_s, wy_r, wp_s, wp_r, wf_s, wf_r,
    dp_s, dp_r, dy_s, dy_r, dq_s, dq_r, tx_s, tx_r, tz_s, tz_r,
):
    n_row, n_col, rb, cb, cap, nkb, toks = dims
    n_y, n_a = n_row // 2, n_col // 2
    rows = max(8, rb)
    row, col = lax.axis_index("row"), lax.axis_index("col")
    y, core = row // 2, lax.rem(row, 2)
    a, b = col // 2, lax.rem(col, 2)
    mate = y * 2 + 1 - core
    side = a * 2 + 1 - b
    pairs = cb // 2

    def y_peer(k):
        return lax.rem(y + k, n_y) * 2 + core

    def z_peer(k):
        return lax.rem(a + k, n_a) * 2 + b

    def push(src, dst, ssem, rsem, r, c):
        return pltpu.make_async_remote_copy(
            src_ref=src, dst_ref=dst, send_sem=ssem, recv_sem=rsem,
            device_id=(r, c), device_id_type=MESH,
        )

    loads = [
        [
            pltpu.make_async_copy(src.at[:, :, pl.ds(nb * BLK, BLK)], wt.at[nb], ldsem.at[m, nb])
            for nb in range(cb)
        ]
        for m, (src, wt) in enumerate(((gw, wt_g), (uw, wt_u)))
    ]
    for c in loads[0]:
        c.start()
    load_cot = pltpu.make_async_copy(cot_in, cot, lsem.at[2])

    barrier = pltpu.get_barrier_semaphore()
    for k in range(1, n_row):
        pl.semaphore_signal(barrier, inc=1, device_id=(lax.rem(row + k, n_row), col), device_id_type=MESH)
    for k in range(1, n_a):
        pl.semaphore_signal(barrier, inc=1, device_id=(row, z_peer(k)), device_id_type=MESH)
    pl.semaphore_signal(barrier, inc=1, device_id=(row, side), device_id_type=MESH)
    for i in range(nkb):
        xb[col * nkb + i] = tok[:, i * BLK:(i + 1) * BLK]
    write_table(gm, tabs_v, row, 0, rows, cap)
    write_table(um, tabs_v, row, 1, rows, cap)
    own_tab = pltpu.make_async_copy(tabs_v.at[row], tab_s, lsem.at[1])
    own_tab.start()
    tab_out[...] = tabs_v[row]
    pl.semaphore_wait(barrier, n_row - 1 + n_a)

    tab_copies = []
    for k in range(1, n_row):
        c = push(tabs_v.at[row], tabs_v.at[row], tab_ss.at[k], tab_rs.at[k], lax.rem(row + k, n_row), col)
        c.start()
        tab_copies.append(c)

    def shard(which):
        return xb.at[pl.ds(which * nkb, nkb)]

    xz = []
    for k in range(1, n_a):
        c = push(shard(col), shard(col), xz_s.at[k], xz_r.at[k], row, z_peer(k))
        c.start()
        xz.append(c)
    xp = [push(shard(col), shard(col), xp_s.at[0], xp_r.at[0], row, side)]
    xp[0].start()

    zero = jnp.zeros((BLK, BLK), BF)
    own, par, ys, fs_ = (own_g, own_u), (par_g, par_u), (yg, yu), (fg, fu)
    for m in range(2):
        own[m][0, cap] = zero
        par[m][0, cap] = zero
        for k in range(n_y - 1):
            ys[m][k, cap] = zero
            fs_[m][k, cap] = zero

    own_tab.wait()
    wy = [[], []]
    wp = []
    unroll = min(8, cap)
    for m, wt in enumerate((wt_g, wt_u)):
        for c in loads[m]:
            c.wait()
        if m == 0:
            for c in loads[1]:
                c.start()
        else:
            load_cot.start()

        def pack(i, _, m=m, wt=wt):
            for j in range(unroll):
                s = i * unroll + j
                own[m][0, s] = wt[tab_s[2 * rows + 2 * m + 1, s], tab_s[2 * rows + 2 * m, s]]
            return 0

        lax.fori_loop(0, cap // unroll, pack, 0)
        mine = own[m].at[0, pl.ds(0, cap)]
        for k in range(1, n_y):
            c = push(mine, ys[m].at[k - 1, pl.ds(0, cap)], wy_s.at[m, k], wy_r.at[m, k], y_peer(k), col)
            wy[m].append(c)
            if m == 0:
                c.start()
        c = push(mine, par[m].at[0, pl.ds(0, cap)], wp_s.at[m], wp_r.at[m], mate, col)
        c.start()
        wp.append(c)

    for c in tab_copies:
        c.wait_recv()
    to_smem = pltpu.make_async_copy(tabs_v, tabs, lsem.at[0])
    to_smem.start()
    to_smem.wait()

    for k in range(1, n_a):
        xz[k - 1].wait_recv()
        source = lax.rem(a - k + n_a, n_a) * 2 + b
        c = push(shard(source), shard(source), xp_s.at[k], xp_r.at[k], row, side)
        c.start()
        xp.append(c)
    for c in wy[0]:
        c.wait_send()
    for c in wy[1]:
        c.start()
    for c in xp:
        c.wait_recv()

    def forward(ref, lead, r, m, acc, first):
        def step(i, _):
            x = jnp.concatenate([xb[r * rb + kb] for kb in range(rb)], axis=1)
            for half in range(2):
                p = i * 2 + half
                for kb in range(rb):
                    for q in range(2):
                        slot = tabs[r, m * rows + kb, p * 2 + q]
                        wch[half, kb * BLK:(kb + 1) * BLK, q * BLK:(q + 1) * BLK] = ref[lead, slot]
                d = jnp.dot(x, wch[half], preferred_element_type=F32)
                if first:
                    acc[p] = d
                else:
                    acc[p] += d
            return 0

        lax.fori_loop(0, pairs // 2, step, 0)

    accs = (gv, uv)
    gbs, gtrs = (gb_g, gb_u), (gtr_g, gtr_u)

    def transpose_x(i, _):
        xt[i] = xb[i].astype(F32).T.astype(BF)
        return 0

    def near_own(m):
        forward(own[m], 0, row, m, accs[m], True)

    def near_mate(m):
        wp[m].wait_recv()
        forward(par[m], 0, mate, m, accs[m], False)

    wf = [[], []]

    def far(m):
        for k in range(1, n_y):
            wy[m][k - 1].wait_recv()
            c = push(
                ys[m].at[k - 1, pl.ds(0, cap)], fs_[m].at[k - 1, pl.ds(0, cap)],
                wf_s.at[m, k], wf_r.at[m, k], mate, col,
            )
            c.start()
            wf[m].append(c)
        for k in range(1, n_y):
            source = lax.rem(y - k + n_y, n_y) * 2
            forward(ys[m], k - 1, source + core, m, accs[m], False)
        for c in wf[m]:
            c.wait_recv()
        for k in range(1, n_y):
            source = lax.rem(y - k + n_y, n_y) * 2
            forward(fs_[m], k - 1, source + 1 - core, m, accs[m], False)

    def units(p):
        return pl.ds(pl.multiple_of(p * 2 * BLK, 2 * BLK), 2 * BLK)

    def keep(grad, p, m):
        grad = grad.astype(BF)
        gbs[m][p * 2] = grad[:, :BLK]
        gbs[m][p * 2 + 1] = grad[:, BLK:]
        gtrs[m][units(p), :] = grad.astype(F32).T.astype(BF)

    def gates_up(p, _):
        g = gv[p]
        keep(cot[:, units(p)].astype(F32) * g * jax.nn.sigmoid(g), p, 1)
        return 0

    def gates_gate(p, _):
        g, u = gv[p], uv[p]
        s = jax.nn.sigmoid(g)
        hid[:, units(p)] = (g * s * u).astype(BF)
        keep(cot[:, units(p)].astype(F32) * u * s * (1.0 + g * (1.0 - s)), p, 0)
        return 0

    def weight_grad(r, m, write):
        def step(i, _):
            for j in range(unroll):
                s = i * unroll + j
                kb, nb = tabs[r, 2 * rows + 2 * m, s], tabs[r, 2 * rows + 2 * m + 1, s]
                write(s, jnp.dot(xt[r * rb + kb], gbs[m][nb], preferred_element_type=F32))
            return 0

        lax.fori_loop(0, cap // unroll, step, 0)

    dp, dy = [[], []], [[], []]

    def far_grad_mate(m):
        for k in range(1, n_y):
            def write(s, v):
                sp[m, k - 1, s] = v.astype(BF)

            weight_grad(lax.rem(y + k, n_y) * 2 + 1 - core, m, write)
            c = push(sp.at[m, k - 1], rp.at[m, k - 1], dp_s.at[m, k], dp_r.at[m, k], mate, col)
            c.start()
            dp[m].append(c)

    def far_grad(m):
        for k in range(1, n_y):
            dp[m][k - 1].wait_recv()

            def write(s, v):
                sy[m, k - 1, s] = (v + rp[m, k - 1, s].astype(F32)).astype(BF)

            weight_grad(y_peer(k), m, write)
            c = push(sy.at[m, k - 1], ry.at[m, k - 1], dy_s.at[m, k], dy_r.at[m, k], y_peer(k), col)
            dy[m].append(c)

    near_own(0)
    near_mate(0)
    lax.fori_loop(0, n_row * rb, transpose_x, 0)
    load_cot.wait()
    far(0)
    lax.fori_loop(0, pairs, gates_up, 0)
    far_grad_mate(1)
    near_own(1)
    far_grad(1)
    for c in wy[1]:
        c.wait_send()
    for c in dy[1]:
        c.start()
    near_mate(1)
    far(1)
    lax.fori_loop(0, pairs, gates_gate, 0)
    stores = [pltpu.make_async_copy(hid, hid_out, lsem.at[3])]
    stores[0].start()
    far_grad_mate(0)

    tiles = [(own, 0, row), (par, 0, mate)]
    for k in range(1, n_y):
        source = lax.rem(y - k + n_y, n_y) * 2
        tiles.append((ys, k - 1, source + core))
        tiles.append((fs_, k - 1, source + 1 - core))
    span = min(2, nkb)

    def token_grad(refs, lead, r, half, write):
        def step(i, _):
            total = None
            for m in range(2):
                for q in range(span):
                    for nb in range(cb):
                        kb = half * nkb + i * span + q
                        slot = tabs[r, m * rows + kb, nb]
                        wrow[m, q * BLK:(q + 1) * BLK, nb * BLK:(nb + 1) * BLK] = refs[m][lead, slot]
                d = jnp.dot(wrow[m], gtrs[m][...], preferred_element_type=F32)
                total = d if total is None else total + d
            write(pl.ds(pl.multiple_of(i * span * BLK, span * BLK), span * BLK), total.T)
            return 0

        lax.fori_loop(0, nkb // span, step, 0)

    tx = []
    for i, (refs, lead, r) in enumerate(tiles):
        def write(at, v, r=r):
            sx[r, :, at] = v.astype(BF)

        token_grad(refs, lead, r, 1 - b, write)
        c = push(sx.at[r], rx.at[r], tx_s.at[i], tx_r.at[i], row, side)
        c.start()
        tx.append(c)
        if i == 0:
            far_grad(0)
            for c in dy[0]:
                c.start()

    for i, (refs, lead, r) in enumerate(tiles):
        tx[i].wait_recv()

        def write(at, v, r=r):
            sz[r, :, at] = (v + rx[r, :, at].astype(F32)).astype(BF)

        token_grad(refs, lead, r, b, write)

        @pl.when(r != a)
        def _():
            k = lax.rem(r - a + n_a, n_a)
            push(sz.at[r], rz.at[k], tz_s.at[k], tz_r.at[k], lax.axis_index("row"), r * 2 + b).start()

    dq = []
    for m in (1, 0):
        def write(s, v):
            sq[m, s] = v.astype(BF)

        weight_grad(mate, m, write)
        c = push(sq.at[m], rq.at[m], dq_s.at[m], dq_r.at[m], mate, col)
        c.start()
        dq.append(c)
    for m, c in zip((1, 0), dq):
        c.wait_recv()

        def write(s, v):
            ow[m, s] = (v + rq[m, s].astype(F32)).astype(BF)

        weight_grad(row, m, write)

    def finish(m, out):
        out[cap] = zero
        for c in dy[m]:
            c.wait_recv()

        def step(s, _):
            v = ow[m, s].astype(F32)
            for k in range(n_y - 1):
                v = v + ry[m, k, s].astype(F32)
            out[s] = v.astype(BF)
            return 0

        lax.fori_loop(0, cap, step, 0)

    finish(1, pu)
    stores.append(pltpu.make_async_copy(pu, pu_out, lsem.at[4]))
    stores[1].start()
    tz = [push(sz.at[z], rz.at[k], tz_s.at[k], tz_r.at[k], row, z * 2 + b)
          for k in range(1, n_a) for z in (lax.rem(a + k, n_a),)]
    total = sz[a].astype(F32)
    for k in range(1, n_a):
        tz[k - 1].wait_recv()
        total = total + rz[k].astype(F32)
    gt[...] = total.astype(BF)
    finish(0, pg)
    stores.append(pltpu.make_async_copy(pg, pg_out, lsem.at[5]))
    stores[2].start()

    for group in (tab_copies, xz, xp, wp, wf[0], wf[1], dp[0], dp[1], dy[0], dy[1], dq, tx, tz):
        for c in group:
            c.wait_send()
    for c in stores:
        c.wait()


def expand(cb, rows, tab_s, pg, pu, hid, gt, grad_g, grad_u, hid_out, gt_out):
    i = pl.program_id(0)
    hid_out[...] = hid[...]
    gt_out[...] = gt[...]
    for m, (packed, out) in enumerate(((pg, grad_g), (pu, grad_u))):
        for nb in range(cb):
            out[:, nb * BLK:(nb + 1) * BLK] = packed[tab_s[m * rows + i, nb]]


def body(n_row, n_col, tokens, gate_weight, up_weight, gate_mask, up_mask, cotangent):
    rb, cb = gate_mask.shape
    cap = rb * cb // 4
    toks, feats = tokens.shape
    nkb = feats // BLK
    units = cb * BLK
    rows = max(8, rb)
    n_y, n_a = n_row // 2, n_col // 2
    assert n_col * nkb == n_row * rb and n_a == n_row and cb % 4 == 0

    vm = pl.BlockSpec(memory_space=pltpu.VMEM)
    anyw = pl.BlockSpec(memory_space=pl.ANY)
    sm = pl.BlockSpec(memory_space=pltpu.SMEM)
    V, D = pltpu.VMEM, pltpu.SemaphoreType.DMA
    blocks = lambda *lead: V((*lead, BLK, BLK), BF)
    scratch = [
        blocks(cb, rb), blocks(cb, rb),
        blocks(1, cap + 1), blocks(1, cap + 1), blocks(1, cap + 1), blocks(1, cap + 1),
        blocks(n_y - 1, cap + 1), blocks(n_y - 1, cap + 1),
        blocks(n_y - 1, cap + 1), blocks(n_y - 1, cap + 1),
        V((n_row, 2 * rows + 8, BLK), jnp.int32),
        pltpu.SMEM((2 * rows + 8, BLK), jnp.int32), pltpu.SMEM((n_row, 2 * rows + 8, BLK), jnp.int32),
        V((n_row * rb, toks, BLK), BF), V((n_row * rb, BLK, toks), BF),
        V((cb // 2, toks, 2 * BLK), F32), V((cb // 2, toks, 2 * BLK), F32),
        V((2, rb * BLK, 2 * BLK), BF), V((2, min(2, nkb) * BLK, units), BF),
        V((cb, toks, BLK), BF), V((cb, toks, BLK), BF),
        V((units, toks), BF), V((units, toks), BF),
        V((toks, units), BF), V((toks, units), BF), blocks(cap + 1), blocks(cap + 1),
        blocks(2, n_y - 1, cap), blocks(2, n_y - 1, cap),
        blocks(2, n_y - 1, cap), blocks(2, n_y - 1, cap),
        blocks(2, cap), blocks(2, cap), blocks(2, cap),
        V((n_a, toks, feats), BF), V((n_a, toks, feats), BF),
        V((n_a, toks, feats), BF), V((n_a, toks, feats), BF),
        D((2, cb)), D((6,)), D((n_row,)), D((n_row,)), D((n_a,)), D((n_a,)), D((n_a,)), D((n_a,)),
        D((2, n_y)), D((2, n_y)), D((2,)), D((2,)), D((2, n_y)), D((2, n_y)),
        D((2, n_y)), D((2, n_y)), D((2, n_y)), D((2, n_y)), D((2,)), D((2,)),
        D((n_a,)), D((n_a,)), D((n_a,)), D((n_a,)),
    ]
    dims = (n_row, n_col, rb, cb, cap, nkb, toks)
    packed = jax.ShapeDtypeStruct((cap + 1, BLK, BLK), BF)
    hidden_type = jax.ShapeDtypeStruct((toks, units), BF)
    tokens_type = jax.ShapeDtypeStruct((toks, feats), BF)
    weight_type = jax.ShapeDtypeStruct((rb * BLK, units), BF)
    hidden, grad_tokens, packed_g, packed_u, tab = pl.pallas_call(
        functools.partial(fused, dims),
        out_shape=(
            hidden_type, tokens_type, packed, packed,
            jax.ShapeDtypeStruct((2 * rows + 8, BLK), jnp.int32),
        ),
        in_specs=[vm, anyw, anyw, vm, vm, anyw],
        out_specs=(anyw, vm, anyw, anyw, vm),
        scratch_shapes=scratch,
        compiler_params=pltpu.CompilerParams(
            collective_id=0, has_side_effects=True, vmem_limit_bytes=62 * 1024 * 1024
        ),
        name="fused_layer",
    )(
        tokens, gate_weight.reshape(rb, BLK, units), up_weight.reshape(rb, BLK, units),
        gate_mask, up_mask, cotangent,
    )

    whole = pl.BlockSpec((cap + 1, BLK, BLK), lambda i: (0, 0, 0))
    hid_strip = pl.BlockSpec((toks // rb, units), lambda i: (i, 0))
    gt_strip = pl.BlockSpec((toks // rb, feats), lambda i: (i, 0))
    strip = pl.BlockSpec((BLK, units), lambda i: (i, 0))
    grad_gate, grad_up, hidden, grad_tokens = pl.pallas_call(
        functools.partial(expand, cb, rows),
        grid=(rb,),
        in_specs=[sm, whole, whole, hid_strip, gt_strip],
        out_specs=(strip, strip, hid_strip, gt_strip),
        out_shape=(weight_type, weight_type, hidden_type, tokens_type),
        name="expand_grads",
    )(tab, packed_g, packed_u, hidden, grad_tokens)
    return hidden, grad_tokens, grad_gate, grad_up


def solution(mesh):
    spec = P("row", "col")
    return jax.shard_map(
        functools.partial(body, mesh.shape["row"], mesh.shape["col"]),
        mesh=mesh,
        in_specs=(spec,) * 6,
        out_specs=(spec,) * 4,
        check_vma=False,
    )
```

```python
import functools

import jax
import jax.numpy as jnp
from jax import lax
from jax.experimental import pallas as pl
from jax.experimental.pallas import tpu as pltpu
from jax.sharding import PartitionSpec as P

BLK = 128
MESH = pl.DeviceIdType.MESH
BF = jnp.bfloat16
F32 = jnp.float32


def write_table(mask_ref, table, row, m, rows, cap):
    rb, cb = mask_ref.shape
    mask = mask_ref[...]
    lane = lax.broadcasted_iota(jnp.int32, (rb, BLK), 1)
    sub = lax.broadcasted_iota(jnp.int32, (rb, BLK), 0)
    sub1 = lax.broadcasted_iota(jnp.int32, (rb, 1), 0)
    cols = [mask[:, nb:nb + 1] for nb in range(cb)]
    run = jnp.zeros((rb, 1), jnp.int32)
    before = []
    for c in cols:
        before.append(run)
        run = run + c
    offset = jnp.zeros((rb, 1), jnp.int32)
    for j in range(rb):
        offset = offset + jnp.where(sub1 > j, run[j:j + 1, :], 0)
    pos = jnp.full((rb, BLK), cap, jnp.int32)
    at_kb = jnp.zeros((rb, BLK), jnp.int32)
    at_nb = jnp.zeros((rb, BLK), jnp.int32)
    for nb, c in enumerate(cols):
        slot = jnp.where(c == 1, offset + before[nb], cap)
        pos = jnp.where(lane == nb, slot, pos)
        here = (lane == slot) & (lane < cap)
        at_kb = at_kb + jnp.where(here, sub, 0)
        at_nb = at_nb + jnp.where(here, nb, 0)
    table[row, m * rows:m * rows + rb, :] = pos
    base = 2 * rows + 2 * m
    table[row, base:base + 1, :] = jnp.sum(at_kb, axis=0, keepdims=True)
    table[row, base + 1:base + 2, :] = jnp.sum(at_nb, axis=0, keepdims=True)


def fused(
    dims, tok, gw, uw, gm, um, cot_in, hid_out, gt, pg_out, pu_out, tab_out,
    wt_g, wt_u, own_g, own_u, par_g, par_u, yg, yu, fg, fu, tabs_v, tab_s, tabs,
    xb, xt, gv, uv, wch, wrow, gb_g, gb_u, gtr_g, gtr_u,
    cot, hid, pg, pu, sp, rp, sy, ry, sq, rq, ow, sx, rx, sz, rz,
    ldsem, lsem, tab_ss, tab_rs, xz_s, xz_r, xp_s, xp_r, wy_s, wy_r, wp_s, wp_r, wf_s, wf_r,
    dp_s, dp_r, dy_s, dy_r, dq_s, dq_r, tx_s, tx_r, tz_s, tz_r,
):
    n_row, n_col, rb, cb, cap, nkb, toks = dims
    n_y, n_a = n_row // 2, n_col // 2
    rows = max(8, rb)
    row, col = lax.axis_index("row"), lax.axis_index("col")
    y, core = row // 2, lax.rem(row, 2)
    a, b = col // 2, lax.rem(col, 2)
    mate = y * 2 + 1 - core
    side = a * 2 + 1 - b
    pairs = cb // 2

    def y_peer(k):
        return lax.rem(y + k, n_y) * 2 + core

    def z_peer(k):
        return lax.rem(a + k, n_a) * 2 + b

    def push(src, dst, ssem, rsem, r, c):
        return pltpu.make_async_remote_copy(
            src_ref=src, dst_ref=dst, send_sem=ssem, recv_sem=rsem,
            device_id=(r, c), device_id_type=MESH,
        )

    loads = [
        [
            pltpu.make_async_copy(src.at[:, :, pl.ds(nb * BLK, BLK)], wt.at[nb], ldsem.at[m, nb])
            for nb in range(cb)
        ]
        for m, (src, wt) in enumerate(((gw, wt_g), (uw, wt_u)))
    ]
    for c in loads[0]:
        c.start()
    load_cot = pltpu.make_async_copy(cot_in, cot, lsem.at[2])

    barrier = pltpu.get_barrier_semaphore()
    for k in range(1, n_row):
        pl.semaphore_signal(barrier, inc=1, device_id=(lax.rem(row + k, n_row), col), device_id_type=MESH)
    for k in range(1, n_a):
        pl.semaphore_signal(barrier, inc=1, device_id=(row, z_peer(k)), device_id_type=MESH)
    pl.semaphore_signal(barrier, inc=1, device_id=(row, side), device_id_type=MESH)
    for i in range(nkb):
        xb[col * nkb + i] = tok[:, i * BLK:(i + 1) * BLK]
    write_table(gm, tabs_v, row, 0, rows, cap)
    write_table(um, tabs_v, row, 1, rows, cap)
    own_tab = pltpu.make_async_copy(tabs_v.at[row], tab_s, lsem.at[1])
    own_tab.start()
    tab_out[...] = tabs_v[row]
    pl.semaphore_wait(barrier, n_row - 1 + n_a)

    tab_copies = []
    for k in range(1, n_row):
        c = push(tabs_v.at[row], tabs_v.at[row], tab_ss.at[k], tab_rs.at[k], lax.rem(row + k, n_row), col)
        c.start()
        tab_copies.append(c)

    def shard(which):
        return xb.at[pl.ds(which * nkb, nkb)]

    xz = []
    for k in range(1, n_a):
        c = push(shard(col), shard(col), xz_s.at[k], xz_r.at[k], row, z_peer(k))
        c.start()
        xz.append(c)
    xp = [push(shard(col), shard(col), xp_s.at[0], xp_r.at[0], row, side)]
    xp[0].start()

    zero = jnp.zeros((BLK, BLK), BF)
    own, par, ys, fs_ = (own_g, own_u), (par_g, par_u), (yg, yu), (fg, fu)
    for m in range(2):
        own[m][0, cap] = zero
        par[m][0, cap] = zero
        for k in range(n_y - 1):
            ys[m][k, cap] = zero
            fs_[m][k, cap] = zero

    own_tab.wait()
    wy = [[], []]
    wp = []
    unroll = min(8, cap)
    for m, wt in enumerate((wt_g, wt_u)):
        for c in loads[m]:
            c.wait()
        if m == 0:
            for c in loads[1]:
                c.start()
        else:
            load_cot.start()

        def pack(i, _, m=m, wt=wt):
            for j in range(unroll):
                s = i * unroll + j
                own[m][0, s] = wt[tab_s[2 * rows + 2 * m + 1, s], tab_s[2 * rows + 2 * m, s]]
            return 0

        lax.fori_loop(0, cap // unroll, pack, 0)
        mine = own[m].at[0, pl.ds(0, cap)]
        for k in range(1, n_y):
            c = push(mine, ys[m].at[k - 1, pl.ds(0, cap)], wy_s.at[m, k], wy_r.at[m, k], y_peer(k), col)
            wy[m].append(c)
            if m == 0:
                c.start()
        c = push(mine, par[m].at[0, pl.ds(0, cap)], wp_s.at[m], wp_r.at[m], mate, col)
        c.start()
        wp.append(c)

    for c in tab_copies:
        c.wait_recv()
    to_smem = pltpu.make_async_copy(tabs_v, tabs, lsem.at[0])
    to_smem.start()
    to_smem.wait()

    def forward(ref, lead, r, m, acc, first, part=None):
        count, base = (rb, 0) if part is None else (nkb, part * nkb)

        def step(i, _):
            x = jnp.concatenate([xb[r * rb + base + kb] for kb in range(count)], axis=1)
            for half in range(2):
                p = i * 2 + half
                for kb in range(count):
                    for q in range(2):
                        slot = tabs[r, m * rows + base + kb, p * 2 + q]
                        wch[half, kb * BLK:(kb + 1) * BLK, q * BLK:(q + 1) * BLK] = ref[lead, slot]
                d = jnp.dot(x, wch[half, :count * BLK], preferred_element_type=F32)
                if first:
                    acc[p] = d
                else:
                    acc[p] += d
            return 0

        lax.fori_loop(0, pairs // 2, step, 0)

    accs = (gv, uv)
    gbs, gtrs = (gb_g, gb_u), (gtr_g, gtr_u)

    def turn(which):
        def step(i, _):
            xt[which * nkb + i] = xb[which * nkb + i].astype(F32).T.astype(BF)
            return 0

        lax.fori_loop(0, nkb, step, 0)

    def near_own(m):
        forward(own[m], 0, row, m, accs[m], True)

    def near_mate(m):
        wp[m].wait_recv()
        forward(par[m], 0, mate, m, accs[m], False)

    wf = [[], []]

    def far(m):
        for k in range(1, n_y):
            wy[m][k - 1].wait_recv()
            c = push(
                ys[m].at[k - 1, pl.ds(0, cap)], fs_[m].at[k - 1, pl.ds(0, cap)],
                wf_s.at[m, k], wf_r.at[m, k], mate, col,
            )
            c.start()
            wf[m].append(c)
        for k in range(1, n_y):
            source = lax.rem(y - k + n_y, n_y) * 2
            forward(ys[m], k - 1, source + core, m, accs[m], False)
        for c in wf[m]:
            c.wait_recv()
        for k in range(1, n_y):
            source = lax.rem(y - k + n_y, n_y) * 2
            forward(fs_[m], k - 1, source + 1 - core, m, accs[m], False)

    def units(p):
        return pl.ds(pl.multiple_of(p * 2 * BLK, 2 * BLK), 2 * BLK)

    def keep(grad, p, m):
        grad = grad.astype(BF)
        gbs[m][p * 2] = grad[:, :BLK]
        gbs[m][p * 2 + 1] = grad[:, BLK:]
        gtrs[m][units(p), :] = grad.astype(F32).T.astype(BF)

    def gates_up(p, _):
        g = gv[p]
        keep(cot[:, units(p)].astype(F32) * g * jax.nn.sigmoid(g), p, 1)
        return 0

    def gates_gate(p, _):
        g, u = gv[p], uv[p]
        s = jax.nn.sigmoid(g)
        hid[:, units(p)] = (g * s * u).astype(BF)
        keep(cot[:, units(p)].astype(F32) * u * s * (1.0 + g * (1.0 - s)), p, 0)
        return 0

    def weight_grad(r, m, write):
        def step(i, _):
            for j in range(unroll):
                s = i * unroll + j
                kb, nb = tabs[r, 2 * rows + 2 * m, s], tabs[r, 2 * rows + 2 * m + 1, s]
                write(s, jnp.dot(xt[r * rb + kb], gbs[m][nb], preferred_element_type=F32))
            return 0

        lax.fori_loop(0, cap // unroll, step, 0)

    dp, dy = [[], []], [[], []]

    def far_grad_mate(m):
        for k in range(1, n_y):
            def write(s, v):
                sp[m, k - 1, s] = v.astype(BF)

            weight_grad(lax.rem(y + k, n_y) * 2 + 1 - core, m, write)
            c = push(sp.at[m, k - 1], rp.at[m, k - 1], dp_s.at[m, k], dp_r.at[m, k], mate, col)
            c.start()
            dp[m].append(c)

    def far_grad(m):
        for k in range(1, n_y):
            dp[m][k - 1].wait_recv()

            def write(s, v):
                sy[m, k - 1, s] = (v + rp[m, k - 1, s].astype(F32)).astype(BF)

            weight_grad(y_peer(k), m, write)
            c = push(sy.at[m, k - 1], ry.at[m, k - 1], dy_s.at[m, k], dy_r.at[m, k], y_peer(k), col)
            dy[m].append(c)

    dq = [None, None]

    def own_chip_mate(m):
        def write(s, v):
            sq[m, s] = v.astype(BF)

        weight_grad(mate, m, write)
        dq[m] = push(sq.at[m], rq.at[m], dq_s.at[m], dq_r.at[m], mate, col)
        dq[m].start()

    def own_chip(m):
        dq[m].wait_recv()

        def write(s, v):
            ow[m, s] = (v + rq[m, s].astype(F32)).astype(BF)

        weight_grad(row, m, write)

    turn(col)
    sources = [lax.rem(a - k + n_a, n_a) * 2 for k in range(n_a)]
    for k in range(1, n_a):
        xz[k - 1].wait_recv()
        c = push(shard(sources[k] + b), shard(sources[k] + b), xp_s.at[k], xp_r.at[k], row, side)
        c.start()
        xp.append(c)
    forward(own[0], 0, row, 0, gv, True, b)
    wp[0].wait_recv()
    forward(par[0], 0, mate, 0, gv, False, b)
    for c in wy[0]:
        c.wait_send()
    for c in wy[1]:
        c.start()
    for k in range(1, n_a):
        turn(sources[k] + b)
    for k in range(n_a):
        xp[k].wait_recv()
        turn(sources[k] + 1 - b)
    forward(own[0], 0, row, 0, gv, False, 1 - b)
    forward(par[0], 0, mate, 0, gv, False, 1 - b)
    load_cot.wait()
    far(0)
    lax.fori_loop(0, pairs, gates_up, 0)
    far_grad_mate(1)
    near_own(1)
    far_grad(1)
    for c in wy[1]:
        c.wait_send()
    for c in dy[1]:
        c.start()
    own_chip_mate(1)
    near_mate(1)
    own_chip(1)
    far(1)
    lax.fori_loop(0, pairs, gates_gate, 0)
    stores = [pltpu.make_async_copy(hid, hid_out, lsem.at[3])]
    stores[0].start()
    far_grad_mate(0)
    own_chip_mate(0)
    far_grad(0)
    for c in dy[0]:
        c.start()

    tiles = [(own, 0, row), (par, 0, mate)]
    for k in range(1, n_y):
        source = lax.rem(y - k + n_y, n_y) * 2
        tiles.append((ys, k - 1, source + core))
        tiles.append((fs_, k - 1, source + 1 - core))
    span = min(2, nkb)

    def token_grad(refs, lead, r, half, write):
        def step(i, _):
            total = None
            for m in range(2):
                for q in range(span):
                    for nb in range(cb):
                        kb = half * nkb + i * span + q
                        slot = tabs[r, m * rows + kb, nb]
                        wrow[m, q * BLK:(q + 1) * BLK, nb * BLK:(nb + 1) * BLK] = refs[m][lead, slot]
                d = jnp.dot(wrow[m], gtrs[m][...], preferred_element_type=F32)
                total = d if total is None else total + d
            write(pl.ds(pl.multiple_of(i * span * BLK, span * BLK), span * BLK), total.T)
            return 0

        lax.fori_loop(0, nkb // span, step, 0)

    tx = []
    for i, (refs, lead, r) in enumerate(tiles):
        def write(at, v, r=r):
            sx[r, :, at] = v.astype(BF)

        token_grad(refs, lead, r, 1 - b, write)
        c = push(sx.at[r], rx.at[r], tx_s.at[i], tx_r.at[i], row, side)
        c.start()
        tx.append(c)

    for i, (refs, lead, r) in enumerate(tiles):
        tx[i].wait_recv()

        def write(at, v, r=r):
            sz[r, :, at] = (v + rx[r, :, at].astype(F32)).astype(BF)

        token_grad(refs, lead, r, b, write)

        @pl.when(r != a)
        def _():
            k = lax.rem(r - a + n_a, n_a)
            push(sz.at[r], rz.at[k], tz_s.at[k], tz_r.at[k], lax.axis_index("row"), r * 2 + b).start()

    own_chip(0)

    def finish(m, out):
        out[cap] = zero
        for c in dy[m]:
            c.wait_recv()

        def step(s, _):
            v = ow[m, s].astype(F32)
            for k in range(n_y - 1):
                v = v + ry[m, k, s].astype(F32)
            out[s] = v.astype(BF)
            return 0

        lax.fori_loop(0, cap, step, 0)

    finish(1, pu)
    stores.append(pltpu.make_async_copy(pu, pu_out, lsem.at[4]))
    stores[1].start()
    tz = [push(sz.at[z], rz.at[k], tz_s.at[k], tz_r.at[k], row, z * 2 + b)
          for k in range(1, n_a) for z in (lax.rem(a + k, n_a),)]
    total = sz[a].astype(F32)
    for k in range(1, n_a):
        tz[k - 1].wait_recv()
        total = total + rz[k].astype(F32)
    gt[...] = total.astype(BF)
    finish(0, pg)
    stores.append(pltpu.make_async_copy(pg, pg_out, lsem.at[5]))
    stores[2].start()

    for group in (tab_copies, xz, xp, wp, wf[0], wf[1], dp[0], dp[1], dy[0], dy[1], dq, tx, tz):
        for c in group:
            c.wait_send()
    for c in stores:
        c.wait()


def expand(cb, rows, tab_s, pg, pu, hid, gt, grad_g, grad_u, hid_out, gt_out):
    i = pl.program_id(0)
    hid_out[...] = hid[...]
    gt_out[...] = gt[...]
    for m, (packed, out) in enumerate(((pg, grad_g), (pu, grad_u))):
        for nb in range(cb):
            out[:, nb * BLK:(nb + 1) * BLK] = packed[tab_s[m * rows + i, nb]]


def body(n_row, n_col, tokens, gate_weight, up_weight, gate_mask, up_mask, cotangent):
    rb, cb = gate_mask.shape
    cap = rb * cb // 4
    toks, feats = tokens.shape
    nkb = feats // BLK
    units = cb * BLK
    rows = max(8, rb)
    n_y, n_a = n_row // 2, n_col // 2
    assert n_col * nkb == n_row * rb and n_a == n_row and cb % 4 == 0

    vm = pl.BlockSpec(memory_space=pltpu.VMEM)
    anyw = pl.BlockSpec(memory_space=pl.ANY)
    sm = pl.BlockSpec(memory_space=pltpu.SMEM)
    V, D = pltpu.VMEM, pltpu.SemaphoreType.DMA
    blocks = lambda *lead: V((*lead, BLK, BLK), BF)
    scratch = [
        blocks(cb, rb), blocks(cb, rb),
        blocks(1, cap + 1), blocks(1, cap + 1), blocks(1, cap + 1), blocks(1, cap + 1),
        blocks(n_y - 1, cap + 1), blocks(n_y - 1, cap + 1),
        blocks(n_y - 1, cap + 1), blocks(n_y - 1, cap + 1),
        V((n_row, 2 * rows + 8, BLK), jnp.int32),
        pltpu.SMEM((2 * rows + 8, BLK), jnp.int32), pltpu.SMEM((n_row, 2 * rows + 8, BLK), jnp.int32),
        V((n_row * rb, toks, BLK), BF), V((n_row * rb, BLK, toks), BF),
        V((cb // 2, toks, 2 * BLK), F32), V((cb // 2, toks, 2 * BLK), F32),
        V((2, rb * BLK, 2 * BLK), BF), V((2, min(2, nkb) * BLK, units), BF),
        V((cb, toks, BLK), BF), V((cb, toks, BLK), BF),
        V((units, toks), BF), V((units, toks), BF),
        V((toks, units), BF), V((toks, units), BF), blocks(cap + 1), blocks(cap + 1),
        blocks(2, n_y - 1, cap), blocks(2, n_y - 1, cap),
        blocks(2, n_y - 1, cap), blocks(2, n_y - 1, cap),
        blocks(2, cap), blocks(2, cap), blocks(2, cap),
        V((n_a, toks, feats), BF), V((n_a, toks, feats), BF),
        V((n_a, toks, feats), BF), V((n_a, toks, feats), BF),
        D((2, cb)), D((6,)), D((n_row,)), D((n_row,)), D((n_a,)), D((n_a,)), D((n_a,)), D((n_a,)),
        D((2, n_y)), D((2, n_y)), D((2,)), D((2,)), D((2, n_y)), D((2, n_y)),
        D((2, n_y)), D((2, n_y)), D((2, n_y)), D((2, n_y)), D((2,)), D((2,)),
        D((n_a,)), D((n_a,)), D((n_a,)), D((n_a,)),
    ]
    dims = (n_row, n_col, rb, cb, cap, nkb, toks)
    packed = jax.ShapeDtypeStruct((cap + 1, BLK, BLK), BF)
    hidden_type = jax.ShapeDtypeStruct((toks, units), BF)
    tokens_type = jax.ShapeDtypeStruct((toks, feats), BF)
    weight_type = jax.ShapeDtypeStruct((rb * BLK, units), BF)
    hidden, grad_tokens, packed_g, packed_u, tab = pl.pallas_call(
        functools.partial(fused, dims),
        out_shape=(
            hidden_type, tokens_type, packed, packed,
            jax.ShapeDtypeStruct((2 * rows + 8, BLK), jnp.int32),
        ),
        in_specs=[vm, anyw, anyw, vm, vm, anyw],
        out_specs=(anyw, vm, anyw, anyw, vm),
        scratch_shapes=scratch,
        compiler_params=pltpu.CompilerParams(
            collective_id=0, has_side_effects=True, vmem_limit_bytes=62 * 1024 * 1024
        ),
        name="fused_layer",
    )(
        tokens, gate_weight.reshape(rb, BLK, units), up_weight.reshape(rb, BLK, units),
        gate_mask, up_mask, cotangent,
    )

    whole = pl.BlockSpec((cap + 1, BLK, BLK), lambda i: (0, 0, 0))
    hid_strip = pl.BlockSpec((toks // rb, units), lambda i: (i, 0))
    gt_strip = pl.BlockSpec((toks // rb, feats), lambda i: (i, 0))
    strip = pl.BlockSpec((BLK, units), lambda i: (i, 0))
    grad_gate, grad_up, hidden, grad_tokens = pl.pallas_call(
        functools.partial(expand, cb, rows),
        grid=(rb,),
        in_specs=[sm, whole, whole, hid_strip, gt_strip],
        out_specs=(strip, strip, hid_strip, gt_strip),
        out_shape=(weight_type, weight_type, hidden_type, tokens_type),
        name="expand_grads",
    )(tab, packed_g, packed_u, hidden, grad_tokens)
    return hidden, grad_tokens, grad_gate, grad_up


def solution(mesh):
    spec = P("row", "col")
    return jax.shard_map(
        functools.partial(body, mesh.shape["row"], mesh.shape["col"]),
        mesh=mesh,
        in_specs=(spec,) * 6,
        out_specs=(spec,) * 4,
        check_vma=False,
    )
```

```python
import functools

import jax
import jax.numpy as jnp
from jax import lax
from jax.experimental import pallas as pl
from jax.experimental.pallas import tpu as pltpu
from jax.sharding import PartitionSpec as P

BLK = 128
MESH = pl.DeviceIdType.MESH
BF = jnp.bfloat16
F32 = jnp.float32


def write_table(mask_ref, table, row, m, rows, cap):
    rb, cb = mask_ref.shape
    mask = mask_ref[...]
    lane = lax.broadcasted_iota(jnp.int32, (rb, BLK), 1)
    sub = lax.broadcasted_iota(jnp.int32, (rb, BLK), 0)
    sub1 = lax.broadcasted_iota(jnp.int32, (rb, 1), 0)
    cols = [mask[:, nb:nb + 1] for nb in range(cb)]
    run = jnp.zeros((rb, 1), jnp.int32)
    before = []
    for c in cols:
        before.append(run)
        run = run + c
    offset = jnp.zeros((rb, 1), jnp.int32)
    for j in range(rb):
        offset = offset + jnp.where(sub1 > j, run[j:j + 1, :], 0)
    pos = jnp.full((rb, BLK), cap, jnp.int32)
    at_kb = jnp.zeros((rb, BLK), jnp.int32)
    at_nb = jnp.zeros((rb, BLK), jnp.int32)
    for nb, c in enumerate(cols):
        slot = jnp.where(c == 1, offset + before[nb], cap)
        pos = jnp.where(lane == nb, slot, pos)
        here = (lane == slot) & (lane < cap)
        at_kb = at_kb + jnp.where(here, sub, 0)
        at_nb = at_nb + jnp.where(here, nb, 0)
    table[row, m * rows:m * rows + rb, :] = pos
    base = 2 * rows + 2 * m
    table[row, base:base + 1, :] = jnp.sum(at_kb, axis=0, keepdims=True)
    table[row, base + 1:base + 2, :] = jnp.sum(at_nb, axis=0, keepdims=True)


def fused(
    dims, tok, gw, uw, gm, um, cot_in, hid_out, gt, pg_out, pu_out, tab_out,
    wt_g, wt_u, own_g, own_u, par_g, par_u, yg, yu, fg, fu, tabs_v, tab_s, tabs,
    xb, xt, gv, uv, wch, wrow, gb_g, gb_u, gtr_g, gtr_u,
    cot, hid, pg, pu, sp, rp, sy, ry, sq, rq, ow, sx, rx, sz, rz,
    ldsem, lsem, tab_ss, tab_rs, xz_s, xz_r, xp_s, xp_r, wy_s, wy_r, wp_s, wp_r, wf_s, wf_r,
    dp_s, dp_r, dy_s, dy_r, dq_s, dq_r, tx_s, tx_r, tz_s, tz_r,
):
    n_row, n_col, rb, cb, cap, nkb, toks = dims
    n_y, n_a = n_row // 2, n_col // 2
    rows = max(8, rb)
    row, col = lax.axis_index("row"), lax.axis_index("col")
    y, core = row // 2, lax.rem(row, 2)
    a, b = col // 2, lax.rem(col, 2)
    mate = y * 2 + 1 - core
    side = a * 2 + 1 - b
    pairs = cb // 2

    def y_peer(k):
        return lax.rem(y + k, n_y) * 2 + core

    def z_peer(k):
        return lax.rem(a + k, n_a) * 2 + b

    def push(src, dst, ssem, rsem, r, c):
        return pltpu.make_async_remote_copy(
            src_ref=src, dst_ref=dst, send_sem=ssem, recv_sem=rsem,
            device_id=(r, c), device_id_type=MESH,
        )

    loads = [
        [
            pltpu.make_async_copy(src.at[:, :, pl.ds(nb * BLK, BLK)], wt.at[nb], ldsem.at[m, nb])
            for nb in range(cb)
        ]
        for m, (src, wt) in enumerate(((gw, wt_g), (uw, wt_u)))
    ]
    for c in loads[0]:
        c.start()
    load_cot = pltpu.make_async_copy(cot_in, cot, lsem.at[2])

    barrier = pltpu.get_barrier_semaphore()
    for k in range(1, n_row):
        pl.semaphore_signal(barrier, inc=1, device_id=(lax.rem(row + k, n_row), col), device_id_type=MESH)
    for k in range(1, n_a):
        pl.semaphore_signal(barrier, inc=1, device_id=(row, z_peer(k)), device_id_type=MESH)
    pl.semaphore_signal(barrier, inc=1, device_id=(row, side), device_id_type=MESH)
    for i in range(nkb):
        xb[col * nkb + i] = tok[:, i * BLK:(i + 1) * BLK]
    write_table(gm, tabs_v, row, 0, rows, cap)
    write_table(um, tabs_v, row, 1, rows, cap)
    own_tab = pltpu.make_async_copy(tabs_v.at[row], tab_s, lsem.at[1])
    own_tab.start()
    tab_out[...] = tabs_v[row]
    pl.semaphore_wait(barrier, n_row - 1 + n_a)

    tab_copies = []
    for k in range(1, n_row):
        c = push(tabs_v.at[row], tabs_v.at[row], tab_ss.at[k], tab_rs.at[k], lax.rem(row + k, n_row), col)
        c.start()
        tab_copies.append(c)

    def shard(which):
        return xb.at[pl.ds(which * nkb, nkb)]

    xz = []
    for k in range(1, n_a):
        c = push(shard(col), shard(col), xz_s.at[k], xz_r.at[k], row, z_peer(k))
        c.start()
        xz.append(c)
    xp = [push(shard(col), shard(col), xp_s.at[0], xp_r.at[0], row, side)]
    xp[0].start()

    zero = jnp.zeros((BLK, BLK), BF)
    own, par, ys, fs_ = (own_g, own_u), (par_g, par_u), (yg, yu), (fg, fu)
    for m in range(2):
        own[m][0, cap] = zero
        par[m][0, cap] = zero
        for k in range(n_y - 1):
            ys[m][k, cap] = zero
            fs_[m][k, cap] = zero

    own_tab.wait()
    wy = [[], []]
    wp = []
    unroll = min(8, cap)
    for m, wt in enumerate((wt_g, wt_u)):
        for c in loads[m]:
            c.wait()
        if m == 0:
            for c in loads[1]:
                c.start()
        else:
            load_cot.start()

        def pack(i, _, m=m, wt=wt):
            for j in range(unroll):
                s = i * unroll + j
                own[m][0, s] = wt[tab_s[2 * rows + 2 * m + 1, s], tab_s[2 * rows + 2 * m, s]]
            return 0

        lax.fori_loop(0, cap // unroll, pack, 0)
        mine = own[m].at[0, pl.ds(0, cap)]
        for k in range(1, n_y):
            c = push(mine, ys[m].at[k - 1, pl.ds(0, cap)], wy_s.at[m, k], wy_r.at[m, k], y_peer(k), col)
            wy[m].append(c)
            if m == 0:
                c.start()
        c = push(mine, par[m].at[0, pl.ds(0, cap)], wp_s.at[m], wp_r.at[m], mate, col)
        c.start()
        wp.append(c)

    for c in tab_copies:
        c.wait_recv()
    to_smem = pltpu.make_async_copy(tabs_v, tabs, lsem.at[0])
    to_smem.start()
    to_smem.wait()

    def forward(ref, lead, r, m, acc, first, part=None):
        count, base = (rb, 0) if part is None else (nkb, part * nkb)

        def step(i, _):
            x = jnp.concatenate([xb[r * rb + base + kb] for kb in range(count)], axis=1)
            for half in range(2):
                p = i * 2 + half
                for kb in range(count):
                    for q in range(2):
                        slot = tabs[r, m * rows + base + kb, p * 2 + q]
                        wch[half, kb * BLK:(kb + 1) * BLK, q * BLK:(q + 1) * BLK] = ref[lead, slot]
                d = jnp.dot(x, wch[half, :count * BLK], preferred_element_type=F32)
                if first:
                    acc[p] = d
                else:
                    acc[p] += d
            return 0

        lax.fori_loop(0, pairs // 2, step, 0)

    accs = (gv, uv)
    gbs, gtrs = (gb_g, gb_u), (gtr_g, gtr_u)

    def turn(which):
        def step(i, _):
            xt[which * nkb + i] = xb[which * nkb + i].astype(F32).T.astype(BF)
            return 0

        lax.fori_loop(0, nkb, step, 0)

    def near_own(m):
        forward(own[m], 0, row, m, accs[m], True)

    def near_mate(m):
        wp[m].wait_recv()
        forward(par[m], 0, mate, m, accs[m], False)

    wf = [[], []]

    def far(m):
        for k in range(1, n_y):
            wy[m][k - 1].wait_recv()
            c = push(
                ys[m].at[k - 1, pl.ds(0, cap)], fs_[m].at[k - 1, pl.ds(0, cap)],
                wf_s.at[m, k], wf_r.at[m, k], mate, col,
            )
            c.start()
            wf[m].append(c)
        for k in range(1, n_y):
            source = lax.rem(y - k + n_y, n_y) * 2
            forward(ys[m], k - 1, source + core, m, accs[m], False)
        for c in wf[m]:
            c.wait_recv()
        for k in range(1, n_y):
            source = lax.rem(y - k + n_y, n_y) * 2
            forward(fs_[m], k - 1, source + 1 - core, m, accs[m], False)

    def units(p):
        return pl.ds(pl.multiple_of(p * 2 * BLK, 2 * BLK), 2 * BLK)

    def keep(grad, p, m):
        grad = grad.astype(BF)
        gbs[m][p * 2] = grad[:, :BLK]
        gbs[m][p * 2 + 1] = grad[:, BLK:]
        gtrs[m][units(p), :] = grad.astype(F32).T.astype(BF)

    def gates_up(p, _):
        g = gv[p]
        keep(cot[:, units(p)].astype(F32) * g * jax.nn.sigmoid(g), p, 1)
        return 0

    def gates_gate(p, _):
        g, u = gv[p], uv[p]
        s = jax.nn.sigmoid(g)
        hid[:, units(p)] = (g * s * u).astype(BF)
        keep(cot[:, units(p)].astype(F32) * u * s * (1.0 + g * (1.0 - s)), p, 0)
        return 0

    def weight_grad(r, m, write):
        def step(i, _):
            for j in range(unroll):
                s = i * unroll + j
                kb, nb = tabs[r, 2 * rows + 2 * m, s], tabs[r, 2 * rows + 2 * m + 1, s]
                write(s, jnp.dot(xt[r * rb + kb], gbs[m][nb], preferred_element_type=F32))
            return 0

        lax.fori_loop(0, cap // unroll, step, 0)

    dp, dy = [[], []], [[], []]

    def far_grad_mate(m):
        for k in range(1, n_y):
            def write(s, v):
                sp[m, k - 1, s] = v.astype(BF)

            weight_grad(lax.rem(y + k, n_y) * 2 + 1 - core, m, write)
            c = push(sp.at[m, k - 1], rp.at[m, k - 1], dp_s.at[m, k], dp_r.at[m, k], mate, col)
            c.start()
            dp[m].append(c)

    def far_grad(m):
        for k in range(1, n_y):
            dp[m][k - 1].wait_recv()

            def write(s, v):
                sy[m, k - 1, s] = (v + rp[m, k - 1, s].astype(F32)).astype(BF)

            weight_grad(y_peer(k), m, write)
            c = push(sy.at[m, k - 1], ry.at[m, k - 1], dy_s.at[m, k], dy_r.at[m, k], y_peer(k), col)
            dy[m].append(c)

    dq = [None, None]

    def own_chip_mate(m):
        def write(s, v):
            sq[m, s] = v.astype(BF)

        weight_grad(mate, m, write)
        dq[m] = push(sq.at[m], rq.at[m], dq_s.at[m], dq_r.at[m], mate, col)
        dq[m].start()

    def own_chip(m):
        dq[m].wait_recv()

        def write(s, v):
            ow[m, s] = (v + rq[m, s].astype(F32)).astype(BF)

        weight_grad(row, m, write)

    turn(col)
    sources = [lax.rem(a - k + n_a, n_a) * 2 for k in range(n_a)]
    for k in range(1, n_a):
        xz[k - 1].wait_recv()
        c = push(shard(sources[k] + b), shard(sources[k] + b), xp_s.at[k], xp_r.at[k], row, side)
        c.start()
        xp.append(c)
    forward(own[0], 0, row, 0, gv, True, b)
    wp[0].wait_recv()
    forward(par[0], 0, mate, 0, gv, False, b)
    for c in wy[0]:
        c.wait_send()
    for c in wy[1]:
        c.start()
    for k in range(1, n_a):
        turn(sources[k] + b)
    for k in range(n_a):
        xp[k].wait_recv()
        turn(sources[k] + 1 - b)
    forward(own[0], 0, row, 0, gv, False, 1 - b)
    forward(par[0], 0, mate, 0, gv, False, 1 - b)
    load_cot.wait()
    far(0)
    lax.fori_loop(0, pairs, gates_up, 0)
    far_grad_mate(1)
    near_own(1)
    far_grad(1)
    for c in wy[1]:
        c.wait_send()
    for c in dy[1]:
        c.start()
    near_mate(1)
    far(1)
    lax.fori_loop(0, pairs, gates_gate, 0)
    stores = [pltpu.make_async_copy(hid, hid_out, lsem.at[3])]
    stores[0].start()

    tiles = [(own, 0, row), (par, 0, mate)]
    for k in range(1, n_y):
        source = lax.rem(y - k + n_y, n_y) * 2
        tiles.append((ys, k - 1, source + core))
        tiles.append((fs_, k - 1, source + 1 - core))
    span = min(2, nkb)

    def token_grad(refs, lead, r, half, write):
        def step(i, _):
            total = None
            for m in range(2):
                for q in range(span):
                    for nb in range(cb):
                        kb = half * nkb + i * span + q
                        slot = tabs[r, m * rows + kb, nb]
                        wrow[m, q * BLK:(q + 1) * BLK, nb * BLK:(nb + 1) * BLK] = refs[m][lead, slot]
                d = jnp.dot(wrow[m], gtrs[m][...], preferred_element_type=F32)
                total = d if total is None else total + d
            write(i, pl.ds(pl.multiple_of(i * span * BLK, span * BLK), span * BLK), total.T)
            return 0

        lax.fori_loop(0, nkb // span, step, 0)

    pieces = [pl.ds(j * span * BLK, span * BLK) for j in range(nkb // span)]

    def to_side(i, j, r, at):
        return push(sx.at[r, :, at], rx.at[r, :, at], tx_s.at[i, j], tx_r.at[i, j], row, side)

    def to_owner(k, j, z, at):
        return push(sz.at[z, :, at], rz.at[k, :, at], tz_s.at[k, j], tz_r.at[k, j], row, z * 2 + b)

    for i, (refs, lead, r) in enumerate(tiles):
        def write(j, at, v, i=i, r=r):
            sx[r, :, at] = v.astype(BF)
            to_side(i, j, r, at).start()

        token_grad(refs, lead, r, 1 - b, write)
        if i == 0:
            far_grad_mate(0)
        if i == 1:
            far_grad(0)
            for c in dy[0]:
                c.start()

    for i, (refs, lead, r) in enumerate(tiles):
        def write(j, at, v, i=i, r=r):
            to_side(i, j, r, at).wait_recv()
            sz[r, :, at] = (v + rx[r, :, at].astype(F32)).astype(BF)

            @pl.when(r != a)
            def _():
                to_owner(lax.rem(r - a + n_a, n_a), j, r, at).start()

        token_grad(refs, lead, r, b, write)

    tx = [to_side(i, j, r, at) for i, (_, _, r) in enumerate(tiles) for j, at in enumerate(pieces)]
    own_chip_mate(1)
    own_chip_mate(0)
    own_chip(1)
    own_chip(0)

    def finish(m, out):
        out[cap] = zero
        for c in dy[m]:
            c.wait_recv()

        def step(s, _):
            v = ow[m, s].astype(F32)
            for k in range(n_y - 1):
                v = v + ry[m, k, s].astype(F32)
            out[s] = v.astype(BF)
            return 0

        lax.fori_loop(0, cap, step, 0)

    finish(1, pu)
    stores.append(pltpu.make_async_copy(pu, pu_out, lsem.at[4]))
    stores[1].start()
    tz = []
    total = sz[a].astype(F32)
    for k in range(1, n_a):
        for j, at in enumerate(pieces):
            tz.append(to_owner(k, j, lax.rem(a + k, n_a), at))
            tz[-1].wait_recv()
        total = total + rz[k].astype(F32)
    gt[...] = total.astype(BF)
    finish(0, pg)
    stores.append(pltpu.make_async_copy(pg, pg_out, lsem.at[5]))
    stores[2].start()

    for group in (tab_copies, xz, xp, wp, wf[0], wf[1], dp[0], dp[1], dy[0], dy[1], dq, tx, tz):
        for c in group:
            c.wait_send()
    for c in stores:
        c.wait()


def expand(cb, rows, tab_s, pg, pu, hid, gt, grad_g, grad_u, hid_out, gt_out):
    i = pl.program_id(0)
    hid_out[...] = hid[...]
    gt_out[...] = gt[...]
    for m, (packed, out) in enumerate(((pg, grad_g), (pu, grad_u))):
        for nb in range(cb):
            out[:, nb * BLK:(nb + 1) * BLK] = packed[tab_s[m * rows + i, nb]]


def body(n_row, n_col, tokens, gate_weight, up_weight, gate_mask, up_mask, cotangent):
    rb, cb = gate_mask.shape
    cap = rb * cb // 4
    toks, feats = tokens.shape
    nkb = feats // BLK
    units = cb * BLK
    rows = max(8, rb)
    n_y, n_a = n_row // 2, n_col // 2
    assert n_col * nkb == n_row * rb and n_a == n_row and cb % 4 == 0

    vm = pl.BlockSpec(memory_space=pltpu.VMEM)
    anyw = pl.BlockSpec(memory_space=pl.ANY)
    sm = pl.BlockSpec(memory_space=pltpu.SMEM)
    V, D = pltpu.VMEM, pltpu.SemaphoreType.DMA
    blocks = lambda *lead: V((*lead, BLK, BLK), BF)
    scratch = [
        blocks(cb, rb), blocks(cb, rb),
        blocks(1, cap + 1), blocks(1, cap + 1), blocks(1, cap + 1), blocks(1, cap + 1),
        blocks(n_y - 1, cap + 1), blocks(n_y - 1, cap + 1),
        blocks(n_y - 1, cap + 1), blocks(n_y - 1, cap + 1),
        V((n_row, 2 * rows + 8, BLK), jnp.int32),
        pltpu.SMEM((2 * rows + 8, BLK), jnp.int32), pltpu.SMEM((n_row, 2 * rows + 8, BLK), jnp.int32),
        V((n_row * rb, toks, BLK), BF), V((n_row * rb, BLK, toks), BF),
        V((cb // 2, toks, 2 * BLK), F32), V((cb // 2, toks, 2 * BLK), F32),
        V((2, rb * BLK, 2 * BLK), BF), V((2, min(2, nkb) * BLK, units), BF),
        V((cb, toks, BLK), BF), V((cb, toks, BLK), BF),
        V((units, toks), BF), V((units, toks), BF),
        V((toks, units), BF), V((toks, units), BF), blocks(cap + 1), blocks(cap + 1),
        blocks(2, n_y - 1, cap), blocks(2, n_y - 1, cap),
        blocks(2, n_y - 1, cap), blocks(2, n_y - 1, cap),
        blocks(2, cap), blocks(2, cap), blocks(2, cap),
        V((n_a, toks, feats), BF), V((n_a, toks, feats), BF),
        V((n_a, toks, feats), BF), V((n_a, toks, feats), BF),
        D((2, cb)), D((6,)), D((n_row,)), D((n_row,)), D((n_a,)), D((n_a,)), D((n_a,)), D((n_a,)),
        D((2, n_y)), D((2, n_y)), D((2,)), D((2,)), D((2, n_y)), D((2, n_y)),
        D((2, n_y)), D((2, n_y)), D((2, n_y)), D((2, n_y)), D((2,)), D((2,)),
        D((n_a, nkb)), D((n_a, nkb)), D((n_a, nkb)), D((n_a, nkb)),
    ]
    dims = (n_row, n_col, rb, cb, cap, nkb, toks)
    packed = jax.ShapeDtypeStruct((cap + 1, BLK, BLK), BF)
    hidden_type = jax.ShapeDtypeStruct((toks, units), BF)
    tokens_type = jax.ShapeDtypeStruct((toks, feats), BF)
    weight_type = jax.ShapeDtypeStruct((rb * BLK, units), BF)
    hidden, grad_tokens, packed_g, packed_u, tab = pl.pallas_call(
        functools.partial(fused, dims),
        out_shape=(
            hidden_type, tokens_type, packed, packed,
            jax.ShapeDtypeStruct((2 * rows + 8, BLK), jnp.int32),
        ),
        in_specs=[vm, anyw, anyw, vm, vm, anyw],
        out_specs=(anyw, vm, anyw, anyw, vm),
        scratch_shapes=scratch,
        compiler_params=pltpu.CompilerParams(
            collective_id=0, has_side_effects=True, vmem_limit_bytes=62 * 1024 * 1024
        ),
        name="fused_layer",
    )(
        tokens, gate_weight.reshape(rb, BLK, units), up_weight.reshape(rb, BLK, units),
        gate_mask, up_mask, cotangent,
    )

    whole = pl.BlockSpec((cap + 1, BLK, BLK), lambda i: (0, 0, 0))
    hid_strip = pl.BlockSpec((toks // rb, units), lambda i: (i, 0))
    gt_strip = pl.BlockSpec((toks // rb, feats), lambda i: (i, 0))
    strip = pl.BlockSpec((BLK, units), lambda i: (i, 0))
    grad_gate, grad_up, hidden, grad_tokens = pl.pallas_call(
        functools.partial(expand, cb, rows),
        grid=(rb,),
        in_specs=[sm, whole, whole, hid_strip, gt_strip],
        out_specs=(strip, strip, hid_strip, gt_strip),
        out_shape=(weight_type, weight_type, hidden_type, tokens_type),
        name="expand_grads",
    )(tab, packed_g, packed_u, hidden, grad_tokens)
    return hidden, grad_tokens, grad_gate, grad_up


def solution(mesh):
    spec = P("row", "col")
    return jax.shard_map(
        functools.partial(body, mesh.shape["row"], mesh.shape["col"]),
        mesh=mesh,
        in_specs=(spec,) * 6,
        out_specs=(spec,) * 4,
        check_vma=False,
    )
```
